32 devices in a mesh: dp: 8 (over z, y), ctx: 4 (over x, core).
Axes of the slice: x: 2, y: 2, z: 4, core: 2. Of those that a mesh axis runs over, the one named last changes fastest.
Arguments:
- queries: bfloat16 [8192, 512], P(('dp', 'ctx')), may hold values from -6 to 6
- key_rows: bfloat16 [8192, 512], P(('dp', 'ctx')), may hold values from -6 to 6
- value_rows: bfloat16 [8192, 512], P(('dp', 'ctx')), may hold values from -6 to 6
- grad_out: bfloat16 [8192, 512], P(('dp', 'ctx')), may hold values from -192 to 192
- rab_table: float32 [4, 13], replicated, may hold values from -1 to 1
- first_block: int32 [8, 4], P('dp'), may hold values from 0 to 3, as said below
- block_fill: int32 [8, 4], P('dp'), may hold values from 1 to 256, as said below
- block_order: int32 [8, 4], P('dp'), may hold values from 0 to 3, each once within a row
Outputs:
- grad_query: bfloat16 [8192, 512], P(('dp', 'ctx'))
- grad_key: bfloat16 [8192, 512], P(('dp', 'ctx'))
- grad_value: bfloat16 [8192, 512], P(('dp', 'ctx'))
- grad_rab: float32 [4, 13], replicated
The draws below stay inside these ranges and needn't reach their ends.
Inputs may be any that keep to these rules, and one draw needn't show every extreme that they name: `block_order`: in each group every number appears once. `first_block`: each history covers consecutive logical blocks of its group, and an entry names the first of them. Logical block 0 starts a history that also covers block 1. Where a group has three or more blocks, its last logical block starts a history of its own. `block_fill`: valid events are the first ones of a block; every block but the last of its history has all 256.
All inputs are finite; a program needn't handle non-finite values.
Results may differ from the reference program's by a relative error of at most 0.0051.
Values may be sent and summed in bfloat16 or wider, within the bound.
A program may use at most 128 MiB of HBM per device.

```python
import jax
import jax.numpy as jnp
from jax import lax

BLOCK = 256
HEADS = 4
HEAD_DIM = 128
NBUCKET = 13
ALL_ROWS = 8192
N_DP = 8
N_CTX = 4


def history_layout(key):
    start_key, fill_key = jax.random.split(key)
    starts = jax.random.randint(start_key, (N_DP, N_CTX), 0, 16) < 3
    index = jnp.arange(N_CTX, dtype=jnp.int32)
    starts = starts | (index == 0)[None, :]
    if N_CTX >= 3:
        starts = starts | (index == N_CTX - 1)[None, :]
    starts = starts & (index != 1)[None, :]
    marked = jnp.where(starts, index[None, :], 0).astype(jnp.int32)
    head_index = lax.cummax(marked, axis=1)
    following = jnp.concatenate([starts[:, 1:], jnp.ones((N_DP, 1), dtype=jnp.bool_)], axis=1)
    partial_fill = jax.random.randint(fill_key, (N_DP, N_CTX), 1, BLOCK + 1)
    fill_count = jnp.where(following, partial_fill, BLOCK)
    return (head_index.astype(jnp.int32), fill_count.astype(jnp.int32))


def draw_first_block(key, part):
    head_index, fill_count = history_layout(key)
    return head_index


def draw_block_fill(key, part):
    head_index, fill_count = history_layout(key)
    return fill_count


def levels(key, extent, pieces, low, top_value):
    def one(dim, shards_of):
        draws = jax.random.uniform(jax.random.fold_in(jax.random.fold_in(key, 6), dim), (shards_of,), jnp.float32, low / len(pieces), top_value / len(pieces))
        return jnp.repeat(jnp.exp(draws), extent[dim] // shards_of).reshape((-1,) + (1,) * (len(extent) - dim - 1))

    factor_of = one(*pieces[0])
    for cut in pieces[1:]:
        factor_of = factor_of * one(*cut)
    return factor_of


def normal_values(rng, extent, scale, most, cuts=(), kind=jnp.bfloat16):
    gain = levels(rng, extent, cuts, -0.22, 0.18) if cuts else 1.0
    entries = jax.random.normal(rng, extent, jnp.float32) * scale * gain
    return jnp.minimum(jnp.maximum(entries, -most), most).astype(kind)


def setup_inputs(seed: int = 0) -> dict:
    streams_of = jax.random.split(jax.random.key(seed), 9)
    queries = normal_values(streams_of[0], (ALL_ROWS, HEADS * HEAD_DIM), 1.0, 6.0, ((0, 32),))
    key_rows = normal_values(streams_of[1], (ALL_ROWS, HEADS * HEAD_DIM), 1.0, 6.0, ((0, 32),))
    value_rows = normal_values(streams_of[2], (ALL_ROWS, HEADS * HEAD_DIM), 1.0, 6.0, ((0, 32),))
    grad_out = normal_values(streams_of[3], (ALL_ROWS, HEADS * HEAD_DIM), 32.0, 192.0, ((0, 32),))
    rab_table = jnp.clip(jax.random.uniform(streams_of[4], (HEADS, NBUCKET), jnp.float32, -1.0, 1.0), -1.0, 1.0)
    first_block = draw_first_block(jax.random.fold_in(streams_of[8], 71), 0)
    block_fill = draw_block_fill(jax.random.fold_in(streams_of[8], 71), 0)
    block_order = jax.vmap(lambda own: jax.random.permutation(own, N_CTX))(jax.random.split(streams_of[7], N_DP)).reshape((N_DP, N_CTX)).astype(jnp.int32)
    return dict(queries=queries, key_rows=key_rows, value_rows=value_rows, grad_out=grad_out, rab_table=rab_table, first_block=first_block, block_fill=block_fill, block_order=block_order)


def bucket_of(distance, bucket_total):
    result = jnp.zeros(distance.shape, jnp.int32)
    for power in range(1, bucket_total):
        result = result + (distance + 1 >= 2 ** power).astype(jnp.int32)
    return result


def reference(queries, key_rows, value_rows, grad_out, rab_table, first_block, block_fill, block_order):
    events = N_CTX * BLOCK
    feat_width = HEADS * HEAD_DIM
    score_scale = HEAD_DIM ** -0.5

    def one_group(group_args):
        query_group, key_group, value_group, cotan_group, head_block, fill_count, slot_order = group_args
        same_hist = (head_block[:, None] == head_block[None, :]).astype(jnp.int32)
        hist_len = jnp.sum(same_hist * fill_count[None, :], axis=1)
        within = jnp.arange(BLOCK, dtype=jnp.int32)
        positions = (slot_order[:, None] * BLOCK + within[None, :]).reshape(-1)
        hist_ids = jnp.repeat(head_block[slot_order], BLOCK)
        valid_rows = (within[None, :] < fill_count[slot_order][:, None]).reshape(-1)
        inverse_len = 1.0 / jnp.repeat(hist_len[slot_order], BLOCK).astype(jnp.float32)
        query_all = query_group.astype(jnp.float32).reshape(events, HEADS, HEAD_DIM)
        key_all = key_group.astype(jnp.float32).reshape(events, HEADS, HEAD_DIM)
        value_all = value_group.astype(jnp.float32).reshape(events, HEADS, HEAD_DIM)
        cotan_all = cotan_group.astype(jnp.float32).reshape(events, HEADS, HEAD_DIM)

        def query_step(totals, slot):
            key_total, value_total, rab_total = totals
            offset = (slot * BLOCK).astype(jnp.int32)
            query_blk = lax.dynamic_slice_in_dim(query_all, offset, BLOCK, 0)
            cotan_blk = lax.dynamic_slice_in_dim(cotan_all, offset, BLOCK, 0)
            query_pos = lax.dynamic_slice_in_dim(positions, offset, BLOCK, 0)
            query_hist = lax.dynamic_slice_in_dim(hist_ids, offset, BLOCK, 0)
            query_valid = lax.dynamic_slice_in_dim(valid_rows, offset, BLOCK, 0)
            query_inv = lax.dynamic_slice_in_dim(inverse_len, offset, BLOCK, 0)
            live_mask = (query_hist[:, None] == hist_ids[None, :]) & (positions[None, :] <= query_pos[:, None])
            live_mask = live_mask & query_valid[:, None] & valid_rows[None, :]
            live_f = live_mask.astype(jnp.float32)
            bucket = bucket_of(jnp.maximum(query_pos[:, None] - positions[None, :], 0), NBUCKET)
            score_bias = rab_table[:, bucket]
            scores = jnp.einsum('ihd,jhd->hij', query_blk, key_all) * score_scale + score_bias
            sigmoid_s = jax.nn.sigmoid(scores)
            attn = (scores * sigmoid_s * live_f * query_inv[None, :, None]).astype(jnp.bfloat16)
            grad_attn = jnp.einsum('ihd,jhd->hij', cotan_blk, value_all) * live_f * query_inv[None, :, None]
            grad_score = grad_attn * (sigmoid_s * (1.0 + scores * (1.0 - sigmoid_s)))
            score_low = grad_score.astype(jnp.bfloat16).astype(jnp.float32)
            query_grad = jnp.einsum('hij,jhd->ihd', score_low, key_all) * score_scale
            key_total = key_total + jnp.einsum('hij,ihd->jhd', score_low, query_blk) * score_scale
            value_total = value_total + jnp.einsum('hij,ihd->jhd', attn.astype(jnp.float32), cotan_blk)
            rab_terms = jax.ops.segment_sum(grad_score.reshape(HEADS, -1).T, bucket.reshape(-1), num_segments=NBUCKET).T
            return (key_total, value_total, rab_total + rab_terms), query_grad

        start_state = (jnp.zeros((events, HEADS, HEAD_DIM), jnp.float32), jnp.zeros((events, HEADS, HEAD_DIM), jnp.float32), jnp.zeros((HEADS, NBUCKET), jnp.float32))
        totals, query_grads = lax.scan(query_step, start_state, jnp.arange(N_CTX, dtype=jnp.int32))
        return (query_grads.reshape(events, feat_width), totals[0].reshape(events, feat_width), totals[1].reshape(events, feat_width), totals[2])

    results = lax.map(one_group, (queries.reshape(N_DP, events, feat_width), key_rows.reshape(N_DP, events, feat_width), value_rows.reshape(N_DP, events, feat_width), grad_out.reshape(N_DP, events, feat_width), first_block, block_fill, block_order))
    grad_query = results[0].reshape(N_DP * events, feat_width).astype(jnp.bfloat16)
    grad_key = results[1].reshape(N_DP * events, feat_width).astype(jnp.bfloat16)
    grad_value = results[2].reshape(N_DP * events, feat_width).astype(jnp.bfloat16)
    grad_rab = jnp.sum(results[3], axis=0)
    return (grad_query, grad_key, grad_value, grad_rab)
```

```python
import functools

import jax
import jax.numpy as jnp
from jax import lax
from jax.experimental import pallas as pl
from jax.experimental.pallas import tpu as pltpu
from jax.sharding import PartitionSpec as P

MESH = pl.DeviceIdType.MESH
F32 = jnp.float32
BF16 = jnp.bfloat16


def bucket_count(distance, bucket_total):
    value = distance + 1
    result = jnp.zeros(distance.shape, jnp.int32)
    for power in range(1, bucket_total):
        result = result + jnp.where(value >= 2**power, 1, 0).astype(jnp.int32)
    return result


def dot_nt(a, b):
    return lax.dot_general(a, b, (((1,), (1,)), ((), ())), preferred_element_type=F32)


def dot_nn(a, b):
    return lax.dot_general(a, b, (((1,), (0,)), ((), ())), preferred_element_type=F32)


def dot_tn(a, b):
    return lax.dot_general(a, b, (((0,), (0,)), ((), ())), preferred_element_type=F32)


def fused_kernel(
    n_dp,
    head_count,
    bucket_total,
    order_ref,
    first_ref,
    fill_ref,
    q_ref,
    k_ref,
    v_ref,
    d_ref,
    table_ref,
    gq_ref,
    gk_ref,
    gv_ref,
    rab_ref,
    vm,
    dm,
    send1,
    send2,
    base2,
    recv1,
    recv2,
    recv3,
    accq,
    acck,
    accv,
    biasv,
    rabs,
    ctx_slots,
    dp_slots,
    s1_send,
    s1_recv,
    s2_send,
    s2_recv,
    s3_send,
    s3_recv,
    rc_send,
    rc_recv,
    rd_send,
    rd_recv,
):
    rows = q_ref.shape[0]
    dim = q_ref.shape[1] // head_count
    scale = dim ** (-0.5)
    blocks = 4
    dp = lax.axis_index("dp")
    me = lax.axis_index("ctx")
    sib = me + 1 - 2 * (me % 2)
    cross = (me + 2) % 4
    diag = (sib + 2) % 4

    barrier = pltpu.get_barrier_semaphore()
    for step in range(1, blocks):
        pl.semaphore_signal(barrier, inc=1, device_id=(dp, (me + step) % blocks), device_id_type=MESH)
    for step in range(1, n_dp):
        pl.semaphore_signal(barrier, inc=1, device_id=((dp + step) % n_dp, me), device_id_type=MESH)

    last = blocks - 1
    log_me = order_ref[0, me]
    log_sib = order_ref[0, sib]
    log_cross = order_ref[0, cross]
    log_diag = order_ref[0, diag]
    hist_me = first_ref[0, log_me]
    fill_me = fill_ref[0, log_me]
    length = jnp.int32(0)
    for block in range(blocks):
        length = length + jnp.where(first_ref[0, block] == hist_me, fill_ref[0, block], 0)
    inverse = 1.0 / jnp.full((1, rows), length, jnp.int32).astype(F32)

    idle = log_me == last
    with_idle = idle | (log_sib == last)

    row_wide = lax.broadcasted_iota(jnp.int32, (rows, dim), 0)
    row_ok = jnp.where(row_wide < fill_me, 1.0, 0.0).astype(F32).astype(BF16)

    def cols(h):
        return pl.ds(pl.multiple_of(h * dim, dim), dim)

    log_one = jnp.where(log_sib == last, log_diag, log_sib)
    log_two = jnp.where(log_cross == last, log_diag, log_cross)
    early_one = log_me < log_one
    early_two = log_me < log_two

    def prepare(h, carry):
        at = cols(h)
        q_h, k_h = q_ref[:, at], k_ref[:, at]
        v_h, d_h = v_ref[:, at] * row_ok, d_ref[:, at] * row_ok
        vm[:, at] = v_h
        dm[:, at] = d_h
        send1[h, 0] = jnp.where(early_one, k_h, q_h)
        send1[h, 1] = jnp.where(early_one, v_h, d_h)
        base2[h, 0] = jnp.where(early_two, k_h, q_h)
        base2[h, 1] = jnp.where(early_two, v_h, d_h)
        return carry

    lax.fori_loop(0, head_count, prepare, 0)

    pl.semaphore_wait(barrier, blocks - 1 + n_dp - 1)

    def copy1(h):
        return pltpu.make_async_remote_copy(
            src_ref=send1.at[h], dst_ref=recv1.at[h], send_sem=s1_send.at[h], recv_sem=s1_recv.at[h],
            device_id=(dp, sib), device_id_type=MESH)

    def copy2(h):
        return pltpu.make_async_remote_copy(
            src_ref=send2.at[h], dst_ref=recv2.at[h], send_sem=s2_send.at[h], recv_sem=s2_recv.at[h],
            device_id=(dp, cross), device_id_type=MESH)

    def copy3(h):
        return pltpu.make_async_remote_copy(
            src_ref=recv2.at[h], dst_ref=recv3.at[h], send_sem=s3_send.at[h], recv_sem=s3_recv.at[h],
            device_id=(dp, sib), device_id_type=MESH)

    for h in range(head_count):
        copy1(h).start()

    table = table_ref[...]
    lane = lax.broadcasted_iota(jnp.int32, (head_count, 2 * rows), 1)
    offset = jnp.where(lane < rows, -lane, 2 * rows - lane)

    def distance_of(delta):
        return jnp.abs(delta * rows + offset)

    log_a = jnp.where(with_idle, log_diag, log_sib)
    log_b = log_two
    delta_a, delta_b = log_me - log_a, log_me - log_b
    buckets = (
        bucket_count(jnp.maximum(offset, 0), bucket_total),
        bucket_count(distance_of(delta_a), bucket_total),
        bucket_count(distance_of(delta_b), bucket_total),
    )
    for kind in range(3):
        filled = jnp.zeros((head_count, 2 * rows), F32)
        for b in range(bucket_total):
            filled = jnp.where(buckets[kind] == b, table[:, b : b + 1], filled)
        for h in range(head_count):
            biasv[kind, h] = filled[h : h + 1] * 0.5

    for h in range(head_count):
        copy1(h).wait_recv()
        send2[h] = jnp.where(idle, recv1[h], base2[h])
        copy2(h).start()

    i_row = lax.broadcasted_iota(jnp.int32, (rows, rows), 0)
    j_col = lax.broadcasted_iota(jnp.int32, (rows, rows), 1)

    def bias_of(kind, h):
        spread = jnp.broadcast_to(biasv[kind, h], (rows, 2 * rows))
        return pltpu.roll(spread, 0, 1, stride=1, stride_axis=0)[:, :rows]

    lane8 = lax.broadcasted_iota(jnp.int32, (8, rows), 1)

    def by_offset(grad_score):
        low = jnp.zeros((8, rows), F32)
        high = jnp.zeros((8, rows), F32)
        for start in range(0, rows, 8):
            part = grad_score[start : start + 8, :]
            if start == 0:
                low = low + part
            else:
                turned = pltpu.roll(part, rows - start, 1)
                wrapped = lane8 >= rows - start
                low = low + jnp.where(wrapped, 0.0, turned)
                high = high + jnp.where(wrapped, turned, 0.0)
        return low, high

    def pair_terms(score_dot, grad_dot, bias, factor):
        half = score_dot * (scale * 0.5) + bias
        turn = jnp.tanh(half)
        up = 1.0 + turn
        raw = half * up
        attn = raw * factor
        slope = (up + raw * (1.0 - turn)) * (factor * 0.5)
        return attn.astype(BF16), grad_dot * slope

    def own_pair(h):
        at = cols(h)
        q_h, k_h, v_h, d_h = q_ref[:, at], k_ref[:, at], vm[:, at], dm[:, at]
        factor = jnp.where(j_col <= i_row, inverse, 0.0)
        attn, grad_score = pair_terms(dot_nt(q_h, k_h), dot_nt(d_h, v_h), bias_of(0, h), factor)
        low_score = grad_score.astype(BF16)
        accq[h] = dot_nn(low_score, k_h)
        acck[h] = dot_tn(low_score, q_h)
        accv[h] = dot_tn(attn, d_h)
        low, high = by_offset(grad_score)
        rabs[0, h, :, :rows] = low
        rabs[0, h, :, rows:] = high

    def other_pair(kind, h, part0, part1, delta, factor):
        at = cols(h)
        later = delta > 0
        own0 = jnp.where(later, q_ref[:, at], k_ref[:, at])
        own1 = jnp.where(later, dm[:, at], vm[:, at])
        attn, grad_score = pair_terms(dot_nt(own0, part0), dot_nt(own1, part1), bias_of(kind, h), factor)
        term0 = dot_nn(grad_score.astype(BF16), part0)
        term1 = dot_nn(attn, part1)
        low, high = by_offset(grad_score)
        take = jnp.where(later, 1.0, 0.0)
        rabs[kind, h, :, :rows] = low * take
        rabs[kind, h, :, rows:] = high * take
        return jnp.where(later, term0, 0.0), jnp.where(later, 0.0, term0), jnp.where(later, 0.0, term1)

    factor_a = jnp.where(first_ref[0, log_a] == hist_me, inverse, 0.0)
    factor_b = jnp.where(first_ref[0, log_b] == hist_me, inverse, 0.0)
    factor_a = jnp.where(idle, 0.0, factor_a)
    factor_b = jnp.where(idle, 0.0, factor_b)

    def own_step(h, carry):
        own_pair(h)
        return carry

    lax.fori_loop(0, head_count, own_step, 0)

    def other_step(h, carry):
        at = cols(h)
        copy2(h).wait_recv()
        copy3(h).start()
        q_b, k_b, v_b = other_pair(2, h, recv2[h, 0], recv2[h, 1], delta_b, factor_b)
        copy3(h).wait_recv()
        part0 = jnp.where(with_idle, recv3[h, 0], recv1[h, 0])
        part1 = jnp.where(with_idle, recv3[h, 1], recv1[h, 1])
        q_a, k_a, v_a = other_pair(1, h, part0, part1, delta_a, factor_a)
        ok = row_wide < fill_me
        gq_ref[:, at] = ((accq[h] + q_a + q_b) * scale).astype(BF16)
        gk_ref[:, at] = ((acck[h] + k_a + k_b) * scale).astype(BF16)
        gv_ref[:, at] = jnp.where(ok, accv[h] + v_a + v_b, 0.0).astype(BF16)
        return carry

    lax.fori_loop(0, head_count, other_step, 0)

    lane_out = lax.broadcasted_iota(jnp.int32, (head_count, 128), 1)
    lane_sum = lax.broadcasted_iota(jnp.int32, (8, 2 * rows), 1)
    offset_sum = lax.broadcasted_iota(jnp.int32, (8, 2 * rows), 0) - jnp.where(
        lane_sum < rows, lane_sum, lane_sum - 2 * rows
    )
    sum_buckets = (
        bucket_count(jnp.maximum(offset_sum, 0), bucket_total),
        bucket_count(jnp.abs(delta_a * rows + offset_sum), bucket_total),
        bucket_count(jnp.abs(delta_b * rows + offset_sum), bucket_total),
    )
    mine = jnp.zeros((head_count, 128), F32)
    for b in range(bucket_total):
        here = [sum_buckets[kind] == b for kind in range(3)]
        per_head = []
        for h in range(head_count):
            picked = jnp.zeros((8, 2 * rows), F32)
            for kind in range(3):
                picked = picked + jnp.where(here[kind], rabs[kind, h], 0.0)
            per_head.append(jnp.sum(picked, axis=0, keepdims=True))
        sums = jnp.sum(jnp.concatenate(per_head, axis=0), axis=1, keepdims=True)
        mine = jnp.where(lane_out == b, sums, mine)
    ctx_slots[me] = jnp.concatenate([mine, jnp.zeros((8 - head_count, 128), F32)], axis=0)

    def rab_ctx(step, owner):
        return pltpu.make_async_remote_copy(
            src_ref=ctx_slots.at[owner], dst_ref=ctx_slots.at[owner], send_sem=rc_send.at[step],
            recv_sem=rc_recv.at[owner], device_id=(dp, (me + step) % blocks), device_id_type=MESH)

    def rab_dp(step, owner):
        return pltpu.make_async_remote_copy(
            src_ref=dp_slots.at[owner], dst_ref=dp_slots.at[owner], send_sem=rd_send.at[step],
            recv_sem=rd_recv.at[owner], device_id=((dp + step) % n_dp, me), device_id_type=MESH)

    for step in range(1, blocks):
        rab_ctx(step, me).start()
    for step in range(1, blocks):
        rab_ctx(step, (me + step) % blocks).wait_recv()
    total = ctx_slots[0]
    for slot in range(1, blocks):
        total = total + ctx_slots[slot]
    dp_slots[dp] = total
    for step in range(1, n_dp):
        rab_dp(step, dp).start()
    for h in range(head_count):
        copy1(h).wait_send()
        copy2(h).wait_send()
        copy3(h).wait_send()
    for step in range(1, blocks):
        rab_ctx(step, me).wait_send()
    for step in range(1, n_dp):
        rab_dp(step, (dp + step) % n_dp).wait_recv()
    total = dp_slots[0]
    for slot in range(1, n_dp):
        total = total + dp_slots[slot]
    for step in range(1, n_dp):
        rab_dp(step, dp).wait_send()
    rab_ref[...] = total[:head_count, :bucket_total]


def four_block_device(
    n_dp, queries, key_rows, value_rows, grad_out, rab_table, first_block, block_fill, block_order
):
    rows, width = queries.shape
    heads, bucket_total = rab_table.shape
    dim = width // heads
    vmem = pl.BlockSpec(memory_space=pltpu.VMEM)
    smem = pl.BlockSpec(memory_space=pltpu.SMEM)
    out = jax.ShapeDtypeStruct((rows, width), BF16)
    buf = pltpu.VMEM((heads, 2, rows, dim), BF16)
    acc = pltpu.VMEM((heads, rows, dim), F32)
    dma = pltpu.SemaphoreType.DMA
    return pl.pallas_call(
        functools.partial(fused_kernel, n_dp, heads, bucket_total),
        out_shape=(out, out, out, jax.ShapeDtypeStruct((heads, bucket_total), F32)),
        in_specs=[smem] * 3 + [vmem] * 5,
        out_specs=(vmem,) * 4,
        scratch_shapes=[
            pltpu.VMEM((rows, width), BF16),
            pltpu.VMEM((rows, width), BF16),
            buf, buf, buf, buf, buf, buf,
            acc, acc, acc,
            pltpu.VMEM((3, heads, 1, 2 * rows), F32),
            pltpu.VMEM((3, heads, 8, 2 * rows), F32),
            pltpu.VMEM((4, 8, 128), F32),
            pltpu.VMEM((n_dp, 8, 128), F32),
            dma((heads,)), dma((heads,)), dma((heads,)), dma((heads,)), dma((heads,)), dma((heads,)),
            dma((4,)), dma((4,)), dma((n_dp,)), dma((n_dp,)),
        ],
        compiler_params=pltpu.CompilerParams(
            collective_id=0, has_side_effects=True, vmem_limit_bytes=40 * 1024 * 1024
        ),
    )(block_order, first_block, block_fill, queries, key_rows, value_rows, grad_out, rab_table)


def bucket_of(distance, bucket_total):
    value = distance + 1
    guess = jnp.floor(jnp.log2(value.astype(jnp.float32))).astype(jnp.int32)
    guess = jnp.clip(guess, 0, 29)
    guess = guess - (jnp.left_shift(jnp.ones_like(guess), guess) > value).astype(jnp.int32)
    guess = guess + (jnp.left_shift(jnp.ones_like(guess), guess + 1) <= value).astype(jnp.int32)
    return jnp.clip(guess, 0, bucket_total - 1)


def lookup(table, index_rows, table_len):
    chosen = (index_rows[:, None] == jnp.arange(table_len, dtype=jnp.int32)[None, :]).astype(
        jnp.int32
    )
    return jnp.sum(chosen * table[None, :], axis=1)


def live_of(query_info, key_info):
    query_pos, query_hist, query_valid, query_inv = query_info
    key_pos, key_hist, key_valid, key_inv = key_info
    live_mask = (query_hist[:, None] == key_hist[None, :]) & (
        key_pos[None, :] <= query_pos[:, None]
    )
    return live_mask & query_valid[:, None] & key_valid[None, :]


def pair_core(
    query_part, key_part, value_part, cotan_part, query_info, key_info, rab_table, score_scale
):
    live_f = live_of(query_info, key_info).astype(jnp.float32)
    query_inv = query_info[3]
    bucket = bucket_of(
        jnp.maximum(query_info[0][:, None] - key_info[0][None, :], 0), rab_table.shape[1]
    )
    score_bias = jnp.take(rab_table, bucket, axis=1)
    scores = (
        jnp.einsum("ihd,jhd->hij", query_part, key_part, preferred_element_type=jnp.float32)
        * score_scale
        + score_bias
    )
    sigmoid_s = jax.nn.sigmoid(scores)
    attn = scores * sigmoid_s * live_f * query_inv[None, :, None]
    grad_attn = (
        jnp.einsum("ihd,jhd->hij", cotan_part, value_part, preferred_element_type=jnp.float32)
        * live_f
        * query_inv[None, :, None]
    )
    grad_score = grad_attn * (sigmoid_s * (1.0 + scores * (1.0 - sigmoid_s)))
    return (attn, grad_score, bucket)


def bias_terms(grad_score, bucket, bucket_total):
    one_hot = (
        bucket.reshape(-1)[:, None] == jnp.arange(bucket_total, dtype=jnp.int32)[None, :]
    ).astype(jnp.float32)
    flat_grad = grad_score.reshape(grad_score.shape[0], -1)
    return jnp.dot(
        flat_grad, one_hot, precision=lax.Precision.HIGHEST, preferred_element_type=jnp.float32
    )


def scan_device(
    queries, key_rows, value_rows, grad_out, rab_table, first_block, block_fill, block_order
):
    row_count, feat_width = queries.shape
    head_count, bucket_total = rab_table.shape
    head_dim = feat_width // head_count
    score_scale = head_dim ** (-0.5)
    block_total = first_block.shape[1]
    head_block = first_block[0]
    fill_count = block_fill[0]
    slot_order = block_order[0]
    same_hist = (head_block[:, None] == head_block[None, :]).astype(jnp.int32)
    hist_len = jnp.sum(same_hist * fill_count[None, :], axis=1)
    slot_hist = lookup(head_block, slot_order, block_total)
    slot_fill = lookup(fill_count, slot_order, block_total)
    slot_len = lookup(hist_len, slot_order, block_total)

    def make_info(offset, count_rows):
        row_ids = offset + jnp.arange(count_rows, dtype=jnp.int32)
        slot_ids = row_ids // row_count
        within = row_ids - slot_ids * row_count
        logical = lookup(slot_order, slot_ids, block_total)
        positions = logical * row_count + within
        hist_ids = lookup(slot_hist, slot_ids, block_total)
        valid_rows = within < lookup(slot_fill, slot_ids, block_total)
        inverse_len = 1.0 / lookup(slot_len, slot_ids, block_total).astype(jnp.float32)
        return (positions, hist_ids, valid_rows, inverse_len)

    own_info = make_info(lax.axis_index("ctx") * row_count, row_count)
    own_query = queries.reshape(row_count, head_count, head_dim)
    own_key = key_rows.reshape(row_count, head_count, head_dim)
    own_value = value_rows.reshape(row_count, head_count, head_dim)
    own_cotan = grad_out.reshape(row_count, head_count, head_dim)

    def query_side(state, piece_key, piece_value, info):
        count_rows = piece_key.shape[0]
        key_part = piece_key.reshape(count_rows, head_count, head_dim)
        value_part = piece_value.reshape(count_rows, head_count, head_dim)
        query_total, rab_total = state
        attn, grad_score, bucket = pair_core(
            own_query, key_part, value_part, own_cotan, own_info, info, rab_table, score_scale
        )
        score_low = grad_score.astype(jnp.bfloat16)
        query_grad = (
            jnp.einsum("hij,jhd->ihd", score_low, key_part, preferred_element_type=jnp.float32)
            * score_scale
        )
        rab_terms = bias_terms(grad_score, bucket, bucket_total)
        return (query_total + query_grad.reshape(row_count, feat_width), rab_total + rab_terms)

    def key_side(state, piece_query, piece_cotan, info):
        count_rows = piece_query.shape[0]
        query_part = piece_query.reshape(count_rows, head_count, head_dim)
        cotan_part = piece_cotan.reshape(count_rows, head_count, head_dim)
        key_total, value_total = state
        attn, grad_score, bucket = pair_core(
            query_part, own_key, own_value, cotan_part, info, own_info, rab_table, score_scale
        )
        key_grad = (
            jnp.einsum(
                "hij,ihd->jhd",
                grad_score.astype(jnp.bfloat16),
                query_part,
                preferred_element_type=jnp.float32,
            )
            * score_scale
        )
        value_grad = jnp.einsum(
            "hij,ihd->jhd",
            attn.astype(jnp.bfloat16),
            cotan_part,
            preferred_element_type=jnp.float32,
        )
        return (
            key_total + key_grad.reshape(row_count, feat_width),
            value_total + value_grad.reshape(row_count, feat_width),
        )

    zero_rows = jnp.zeros((row_count, feat_width), jnp.float32)
    zero_rab = jnp.zeros((head_count, bucket_total), jnp.float32)

    def tile_all(totals, tiles, info):
        tile_query, tile_key, tile_value, tile_cotan = tiles
        query_state = query_side((totals[0], totals[1]), tile_key, tile_value, info)
        key_state = key_side((totals[2], totals[3]), tile_query, tile_cotan, info)
        return (query_state[0], query_state[1], key_state[0], key_state[1])

    pieces = (
        lax.all_gather(queries, "ctx", axis=0, tiled=True),
        lax.all_gather(key_rows, "ctx", axis=0, tiled=True),
        lax.all_gather(value_rows, "ctx", axis=0, tiled=True),
        lax.all_gather(grad_out, "ctx", axis=0, tiled=True),
    )
    tile_count = pieces[0].shape[0] // row_count
    stacked = tuple((piece.reshape(tile_count, row_count, feat_width) for piece in pieces))

    def step(carry, item):
        tile_index = item[0]
        info = make_info(tile_index * row_count, row_count)
        return (tile_all(carry, item[1:], info), None)

    result, unused = lax.scan(
        step,
        (zero_rows, zero_rab, zero_rows, zero_rows),
        (jnp.arange(tile_count, dtype=jnp.int32),) + stacked,
    )
    totals = result
    query_total, rab_total, key_total, value_total = totals
    grad_rab = lax.psum(rab_total, ("dp", "ctx"))
    return (
        query_total.astype(jnp.bfloat16),
        key_total.astype(jnp.bfloat16),
        value_total.astype(jnp.bfloat16),
        grad_rab,
    )


def solution(mesh):
    if mesh.shape["ctx"] == 4:
        body = functools.partial(four_block_device, mesh.shape["dp"])
    else:
        body = scan_device
    return jax.shard_map(
        body,
        mesh=mesh,
        in_specs=(
            P(("dp", "ctx"), None),
            P(("dp", "ctx"), None),
            P(("dp", "ctx"), None),
            P(("dp", "ctx"), None),
            P(),
            P("dp", None),
            P("dp", None),
            P("dp", None),
        ),
        out_specs=(P(("dp", "ctx"), None), P(("dp", "ctx"), None), P(("dp", "ctx"), None), P()),
        check_vma=False,
    )
```

```python
import functools

import jax
import jax.numpy as jnp
from jax import lax
from jax.experimental import pallas as pl
from jax.experimental.pallas import tpu as pltpu
from jax.sharding import PartitionSpec as P

MESH = pl.DeviceIdType.MESH
F32 = jnp.float32
BF16 = jnp.bfloat16


def bucket_count(distance, bucket_total):
    value = distance + 1
    result = jnp.zeros(distance.shape, jnp.int32)
    for power in range(1, bucket_total):
        result = result + jnp.where(value >= 2**power, 1, 0).astype(jnp.int32)
    return result


def dot_nt(a, b):
    return lax.dot_general(a, b, (((1,), (1,)), ((), ())), preferred_element_type=F32)


def dot_nn(a, b):
    return lax.dot_general(a, b, (((1,), (0,)), ((), ())), preferred_element_type=F32)


def dot_tn(a, b):
    return lax.dot_general(a, b, (((0,), (0,)), ((), ())), preferred_element_type=F32)


def fused_kernel(
    n_dp,
    head_count,
    bucket_total,
    order_hbm,
    first_hbm,
    fill_hbm,
    q_hbm,
    k_hbm,
    v_hbm,
    d_hbm,
    table_hbm,
    gq_ref,
    gk_ref,
    gv_ref,
    rab_ref,
    order_ref,
    first_ref,
    fill_ref,
    q_ref,
    k_ref,
    vm,
    dm,
    table_ref,
    in_sems,
    send1,
    send2,
    base2,
    recv1,
    recv2,
    recv3,
    accq,
    acck,
    accv,
    biasv,
    rabs,
    ctx_slots,
    dp_slots,
    s1_send,
    s1_recv,
    s2_send,
    s2_recv,
    s3_send,
    s3_recv,
    rc_send,
    rc_recv,
    rd_send,
    rd_recv,
):
    fetches = [
        pltpu.make_async_copy(source, target, in_sems.at[index])
        for index, (source, target) in enumerate((
            (order_hbm, order_ref), (first_hbm, first_ref), (fill_hbm, fill_ref), (q_hbm, q_ref),
            (k_hbm, k_ref), (v_hbm, vm), (d_hbm, dm), (table_hbm, table_ref),
        ))
    ]
    for fetch in fetches:
        fetch.start()
    rows = q_ref.shape[0]
    dim = q_ref.shape[1] // head_count
    scale = dim ** (-0.5)
    blocks = 4
    dp = lax.axis_index("dp")
    me = lax.axis_index("ctx")
    sib = me + 1 - 2 * (me % 2)
    cross = (me + 2) % 4
    diag = (sib + 2) % 4

    barrier = pltpu.get_barrier_semaphore()
    for step in range(1, blocks):
        pl.semaphore_signal(barrier, inc=1, device_id=(dp, (me + step) % blocks), device_id_type=MESH)
    for step in range(1, n_dp):
        pl.semaphore_signal(barrier, inc=1, device_id=((dp + step) % n_dp, me), device_id_type=MESH)

    for fetch in fetches:
        fetch.wait()
    pl.semaphore_wait(barrier, blocks - 1 + n_dp - 1)

    last = blocks - 1
    log_me = order_ref[0, me]
    log_sib = order_ref[0, sib]
    log_cross = order_ref[0, cross]
    log_diag = order_ref[0, diag]
    hist_me = first_ref[0, log_me]
    fill_me = fill_ref[0, log_me]
    length = jnp.int32(0)
    for block in range(blocks):
        length = length + jnp.where(first_ref[0, block] == hist_me, fill_ref[0, block], 0)
    inverse = 1.0 / jnp.full((1, rows), length, jnp.int32).astype(F32)

    idle = log_me == last
    with_idle = idle | (log_sib == last)

    row_wide = lax.broadcasted_iota(jnp.int32, (rows, dim), 0)
    row_ok = jnp.where(row_wide < fill_me, 1.0, 0.0).astype(F32).astype(BF16)

    def cols(h):
        return pl.ds(pl.multiple_of(h * dim, dim), dim)

    log_one = jnp.where(log_sib == last, log_diag, log_sib)
    log_two = jnp.where(log_cross == last, log_diag, log_cross)
    early_one = log_me < log_one
    early_two = log_me < log_two

    def prepare(h):
        at = cols(h)
        q_h, k_h = q_ref[:, at], k_ref[:, at]
        v_h, d_h = vm[:, at] * row_ok, dm[:, at] * row_ok
        vm[:, at] = v_h
        dm[:, at] = d_h
        send1[h, 0] = jnp.where(early_one, k_h, q_h)
        send1[h, 1] = jnp.where(early_one, v_h, d_h)
        base2[h, 0] = jnp.where(early_two, k_h, q_h)
        base2[h, 1] = jnp.where(early_two, v_h, d_h)

    def copy1(h):
        return pltpu.make_async_remote_copy(
            src_ref=send1.at[h], dst_ref=recv1.at[h], send_sem=s1_send.at[h], recv_sem=s1_recv.at[h],
            device_id=(dp, sib), device_id_type=MESH)

    def copy2(h):
        return pltpu.make_async_remote_copy(
            src_ref=send2.at[h], dst_ref=recv2.at[h], send_sem=s2_send.at[h], recv_sem=s2_recv.at[h],
            device_id=(dp, cross), device_id_type=MESH)

    def copy3(h):
        return pltpu.make_async_remote_copy(
            src_ref=recv2.at[h], dst_ref=recv3.at[h], send_sem=s3_send.at[h], recv_sem=s3_recv.at[h],
            device_id=(dp, sib), device_id_type=MESH)

    def prepare_and_send(h, carry):
        prepare(h)
        copy1(h).start()
        return carry

    lax.fori_loop(0, head_count, prepare_and_send, 0)

    table = table_ref[...]
    lane = lax.broadcasted_iota(jnp.int32, (head_count, 2 * rows), 1)
    offset = jnp.where(lane < rows, -lane, 2 * rows - lane)

    def distance_of(delta):
        return jnp.abs(delta * rows + offset)

    log_a = jnp.where(with_idle, log_diag, log_sib)
    log_b = log_two
    delta_a, delta_b = log_me - log_a, log_me - log_b
    buckets = (
        bucket_count(jnp.maximum(offset, 0), bucket_total),
        bucket_count(distance_of(delta_a), bucket_total),
        bucket_count(distance_of(delta_b), bucket_total),
    )
    for kind in range(3):
        filled = jnp.zeros((head_count, 2 * rows), F32)
        for b in range(bucket_total):
            filled = jnp.where(buckets[kind] == b, table[:, b : b + 1], filled)
        for h in range(head_count):
            biasv[kind, h] = filled[h : h + 1] * 0.5

    for h in range(head_count):
        copy1(h).wait_recv()
        send2[h] = jnp.where(idle, recv1[h], base2[h])
        copy2(h).start()

    i_row = lax.broadcasted_iota(jnp.int32, (rows, rows), 0)
    j_col = lax.broadcasted_iota(jnp.int32, (rows, rows), 1)

    def bias_of(kind, h):
        spread = jnp.broadcast_to(biasv[kind, h], (rows, 2 * rows))
        return pltpu.roll(spread, 0, 1, stride=1, stride_axis=0)[:, :rows]

    lane8 = lax.broadcasted_iota(jnp.int32, (8, rows), 1)

    def by_offset(grad_score):
        low = jnp.zeros((8, rows), F32)
        high = jnp.zeros((8, rows), F32)
        for start in range(0, rows, 8):
            part = grad_score[start : start + 8, :]
            if start == 0:
                low = low + part
            else:
                turned = pltpu.roll(part, rows - start, 1)
                wrapped = lane8 >= rows - start
                low = low + jnp.where(wrapped, 0.0, turned)
                high = high + jnp.where(wrapped, turned, 0.0)
        return low, high

    def pair_terms(score_dot, grad_dot, bias, factor):
        half = score_dot * (scale * 0.5) + bias
        turn = jnp.tanh(half)
        up = 1.0 + turn
        raw = half * up
        attn = raw * factor
        slope = (up + raw * (1.0 - turn)) * (factor * 0.5)
        return attn.astype(BF16), grad_dot * slope

    def own_pair(h):
        at = cols(h)
        q_h, k_h, v_h, d_h = q_ref[:, at], k_ref[:, at], vm[:, at], dm[:, at]
        factor = jnp.where(j_col <= i_row, inverse, 0.0)
        attn, grad_score = pair_terms(dot_nt(q_h, k_h), dot_nt(d_h, v_h), bias_of(0, h), factor)
        low_score = grad_score.astype(BF16)
        accq[h] = dot_nn(low_score, k_h)
        acck[h] = dot_tn(low_score, q_h)
        accv[h] = dot_tn(attn, d_h)
        low, high = by_offset(grad_score)
        rabs[0, h, :, :rows] = low
        rabs[0, h, :, rows:] = high

    def other_pair(kind, h, part0, part1, delta, factor):
        at = cols(h)
        later = delta > 0
        own0 = jnp.where(later, q_ref[:, at], k_ref[:, at])
        own1 = jnp.where(later, dm[:, at], vm[:, at])
        attn, grad_score = pair_terms(dot_nt(own0, part0), dot_nt(own1, part1), bias_of(kind, h), factor)
        term0 = dot_nn(grad_score.astype(BF16), part0)
        term1 = dot_nn(attn, part1)
        low, high = by_offset(grad_score)
        take = jnp.where(later, 1.0, 0.0)
        rabs[kind, h, :, :rows] = low * take
        rabs[kind, h, :, rows:] = high * take
        return jnp.where(later, term0, 0.0), jnp.where(later, 0.0, term0), jnp.where(later, 0.0, term1)

    factor_a = jnp.where(first_ref[0, log_a] == hist_me, inverse, 0.0)
    factor_b = jnp.where(first_ref[0, log_b] == hist_me, inverse, 0.0)
    factor_a = jnp.where(idle, 0.0, factor_a)
    factor_b = jnp.where(idle, 0.0, factor_b)

    def own_step(h, carry):
        own_pair(h)
        return carry

    lax.fori_loop(0, head_count, own_step, 0)

    def other_step(h, carry):
        at = cols(h)
        copy2(h).wait_recv()
        copy3(h).start()
        q_b, k_b, v_b = other_pair(2, h, recv2[h, 0], recv2[h, 1], delta_b, factor_b)
        copy3(h).wait_recv()
        part0 = jnp.where(with_idle, recv3[h, 0], recv1[h, 0])
        part1 = jnp.where(with_idle, recv3[h, 1], recv1[h, 1])
        q_a, k_a, v_a = other_pair(1, h, part0, part1, delta_a, factor_a)
        ok = row_wide < fill_me
        gq_ref[:, at] = ((accq[h] + q_a + q_b) * scale).astype(BF16)
        gk_ref[:, at] = ((acck[h] + k_a + k_b) * scale).astype(BF16)
        gv_ref[:, at] = jnp.where(ok, accv[h] + v_a + v_b, 0.0).astype(BF16)
        return carry

    lax.fori_loop(0, head_count, other_step, 0)

    lane_out = lax.broadcasted_iota(jnp.int32, (head_count, 128), 1)
    lane_sum = lax.broadcasted_iota(jnp.int32, (8, 2 * rows), 1)
    offset_sum = lax.broadcasted_iota(jnp.int32, (8, 2 * rows), 0) - jnp.where(
        lane_sum < rows, lane_sum, lane_sum - 2 * rows
    )
    sum_buckets = (
        bucket_count(jnp.maximum(offset_sum, 0), bucket_total),
        bucket_count(jnp.abs(delta_a * rows + offset_sum), bucket_total),
        bucket_count(jnp.abs(delta_b * rows + offset_sum), bucket_total),
    )
    mine = jnp.zeros((head_count, 128), F32)
    for b in range(bucket_total):
        here = [sum_buckets[kind] == b for kind in range(3)]
        per_head = []
        for h in range(head_count):
            picked = jnp.zeros((8, 2 * rows), F32)
            for kind in range(3):
                picked = picked + jnp.where(here[kind], rabs[kind, h], 0.0)
            per_head.append(jnp.sum(picked, axis=0, keepdims=True))
        sums = jnp.sum(jnp.concatenate(per_head, axis=0), axis=1, keepdims=True)
        mine = jnp.where(lane_out == b, sums, mine)
    ctx_slots[me] = jnp.concatenate([mine, jnp.zeros((8 - head_count, 128), F32)], axis=0)

    def rab_ctx(step, owner):
        return pltpu.make_async_remote_copy(
            src_ref=ctx_slots.at[owner], dst_ref=ctx_slots.at[owner], send_sem=rc_send.at[step],
            recv_sem=rc_recv.at[owner], device_id=(dp, (me + step) % blocks), device_id_type=MESH)

    def rab_dp(step, owner):
        return pltpu.make_async_remote_copy(
            src_ref=dp_slots.at[owner], dst_ref=dp_slots.at[owner], send_sem=rd_send.at[step],
            recv_sem=rd_recv.at[owner], device_id=((dp + step) % n_dp, me), device_id_type=MESH)

    for step in range(1, blocks):
        rab_ctx(step, me).start()
    for step in range(1, blocks):
        rab_ctx(step, (me + step) % blocks).wait_recv()
    total = ctx_slots[0]
    for slot in range(1, blocks):
        total = total + ctx_slots[slot]
    dp_slots[dp] = total
    for step in range(1, n_dp):
        rab_dp(step, dp).start()
    for h in range(head_count):
        copy1(h).wait_send()
        copy2(h).wait_send()
        copy3(h).wait_send()
    for step in range(1, blocks):
        rab_ctx(step, me).wait_send()
    for step in range(1, n_dp):
        rab_dp(step, (dp + step) % n_dp).wait_recv()
    total = dp_slots[0]
    for slot in range(1, n_dp):
        total = total + dp_slots[slot]
    for step in range(1, n_dp):
        rab_dp(step, dp).wait_send()
    rab_ref[...] = total[:head_count, :bucket_total]


def four_block_device(
    n_dp, queries, key_rows, value_rows, grad_out, rab_table, first_block, block_fill, block_order
):
    rows, width = queries.shape
    heads, bucket_total = rab_table.shape
    dim = width // heads
    vmem = pl.BlockSpec(memory_space=pltpu.VMEM)
    out = jax.ShapeDtypeStruct((rows, width), BF16)
    buf = pltpu.VMEM((heads, 2, rows, dim), BF16)
    acc = pltpu.VMEM((heads, rows, dim), F32)
    dma = pltpu.SemaphoreType.DMA
    return pl.pallas_call(
        functools.partial(fused_kernel, n_dp, heads, bucket_total),
        out_shape=(out, out, out, jax.ShapeDtypeStruct((heads, bucket_total), F32)),
        in_specs=[pl.BlockSpec(memory_space=pltpu.HBM)] * 8,
        out_specs=(vmem,) * 4,
        scratch_shapes=[
            pltpu.SMEM(block_order.shape, jnp.int32),
            pltpu.SMEM(first_block.shape, jnp.int32),
            pltpu.SMEM(block_fill.shape, jnp.int32),
            pltpu.VMEM((rows, width), BF16),
            pltpu.VMEM((rows, width), BF16),
            pltpu.VMEM((rows, width), BF16),
            pltpu.VMEM((rows, width), BF16),
            pltpu.VMEM(rab_table.shape, F32),
            dma((8,)),
            buf, buf, buf, buf, buf, buf,
            acc, acc, acc,
            pltpu.VMEM((3, heads, 1, 2 * rows), F32),
            pltpu.VMEM((3, heads, 8, 2 * rows), F32),
            pltpu.VMEM((4, 8, 128), F32),
            pltpu.VMEM((n_dp, 8, 128), F32),
            dma((heads,)), dma((heads,)), dma((heads,)), dma((heads,)), dma((heads,)), dma((heads,)),
            dma((4,)), dma((4,)), dma((n_dp,)), dma((n_dp,)),
        ],
        compiler_params=pltpu.CompilerParams(
            collective_id=0, has_side_effects=True
        ),
    )(block_order, first_block, block_fill, queries, key_rows, value_rows, grad_out, rab_table)


def bucket_of(distance, bucket_total):
    value = distance + 1
    guess = jnp.floor(jnp.log2(value.astype(jnp.float32))).astype(jnp.int32)
    guess = jnp.clip(guess, 0, 29)
    guess = guess - (jnp.left_shift(jnp.ones_like(guess), guess) > value).astype(jnp.int32)
    guess = guess + (jnp.left_shift(jnp.ones_like(guess), guess + 1) <= value).astype(jnp.int32)
    return jnp.clip(guess, 0, bucket_total - 1)


def lookup(table, index_rows, table_len):
    chosen = (index_rows[:, None] == jnp.arange(table_len, dtype=jnp.int32)[None, :]).astype(
        jnp.int32
    )
    return jnp.sum(chosen * table[None, :], axis=1)


def live_of(query_info, key_info):
    query_pos, query_hist, query_valid, query_inv = query_info
    key_pos, key_hist, key_valid, key_inv = key_info
    live_mask = (query_hist[:, None] == key_hist[None, :]) & (
        key_pos[None, :] <= query_pos[:, None]
    )
    return live_mask & query_valid[:, None] & key_valid[None, :]


def pair_core(
    query_part, key_part, value_part, cotan_part, query_info, key_info, rab_table, score_scale
):
    live_f = live_of(query_info, key_info).astype(jnp.float32)
    query_inv = query_info[3]
    bucket = bucket_of(
        jnp.maximum(query_info[0][:, None] - key_info[0][None, :], 0), rab_table.shape[1]
    )
    score_bias = jnp.take(rab_table, bucket, axis=1)
    scores = (
        jnp.einsum("ihd,jhd->hij", query_part, key_part, preferred_element_type=jnp.float32)
        * score_scale
        + score_bias
    )
    sigmoid_s = jax.nn.sigmoid(scores)
    attn = scores * sigmoid_s * live_f * query_inv[None, :, None]
    grad_attn = (
        jnp.einsum("ihd,jhd->hij", cotan_part, value_part, preferred_element_type=jnp.float32)
        * live_f
        * query_inv[None, :, None]
    )
    grad_score = grad_attn * (sigmoid_s * (1.0 + scores * (1.0 - sigmoid_s)))
    return (attn, grad_score, bucket)


def bias_terms(grad_score, bucket, bucket_total):
    one_hot = (
        bucket.reshape(-1)[:, None] == jnp.arange(bucket_total, dtype=jnp.int32)[None, :]
    ).astype(jnp.float32)
    flat_grad = grad_score.reshape(grad_score.shape[0], -1)
    return jnp.dot(
        flat_grad, one_hot, precision=lax.Precision.HIGHEST, preferred_element_type=jnp.float32
    )


def scan_device(
    queries, key_rows, value_rows, grad_out, rab_table, first_block, block_fill, block_order
):
    row_count, feat_width = queries.shape
    head_count, bucket_total = rab_table.shape
    head_dim = feat_width // head_count
    score_scale = head_dim ** (-0.5)
    block_total = first_block.shape[1]
    head_block = first_block[0]
    fill_count = block_fill[0]
    slot_order = block_order[0]
    same_hist = (head_block[:, None] == head_block[None, :]).astype(jnp.int32)
    hist_len = jnp.sum(same_hist * fill_count[None, :], axis=1)
    slot_hist = lookup(head_block, slot_order, block_total)
    slot_fill = lookup(fill_count, slot_order, block_total)
    slot_len = lookup(hist_len, slot_order, block_total)

    def make_info(offset, count_rows):
        row_ids = offset + jnp.arange(count_rows, dtype=jnp.int32)
        slot_ids = row_ids // row_count
        within = row_ids - slot_ids * row_count
        logical = lookup(slot_order, slot_ids, block_total)
        positions = logical * row_count + within
        hist_ids = lookup(slot_hist, slot_ids, block_total)
        valid_rows = within < lookup(slot_fill, slot_ids, block_total)
        inverse_len = 1.0 / lookup(slot_len, slot_ids, block_total).astype(jnp.float32)
        return (positions, hist_ids, valid_rows, inverse_len)

    own_info = make_info(lax.axis_index("ctx") * row_count, row_count)
    own_query = queries.reshape(row_count, head_count, head_dim)
    own_key = key_rows.reshape(row_count, head_count, head_dim)
    own_value = value_rows.reshape(row_count, head_count, head_dim)
    own_cotan = grad_out.reshape(row_count, head_count, head_dim)

    def query_side(state, piece_key, piece_value, info):
        count_rows = piece_key.shape[0]
        key_part = piece_key.reshape(count_rows, head_count, head_dim)
        value_part = piece_value.reshape(count_rows, head_count, head_dim)
        query_total, rab_total = state
        attn, grad_score, bucket = pair_core(
            own_query, key_part, value_part, own_cotan, own_info, info, rab_table, score_scale
        )
        score_low = grad_score.astype(jnp.bfloat16)
        query_grad = (
            jnp.einsum("hij,jhd->ihd", score_low, key_part, preferred_element_type=jnp.float32)
            * score_scale
        )
        rab_terms = bias_terms(grad_score, bucket, bucket_total)
        return (query_total + query_grad.reshape(row_count, feat_width), rab_total + rab_terms)

    def key_side(state, piece_query, piece_cotan, info):
        count_rows = piece_query.shape[0]
        query_part = piece_query.reshape(count_rows, head_count, head_dim)
        cotan_part = piece_cotan.reshape(count_rows, head_count, head_dim)
        key_total, value_total = state
        attn, grad_score, bucket = pair_core(
            query_part, own_key, own_value, cotan_part, info, own_info, rab_table, score_scale
        )
        key_grad = (
            jnp.einsum(
                "hij,ihd->jhd",
                grad_score.astype(jnp.bfloat16),
                query_part,
                preferred_element_type=jnp.float32,
            )
            * score_scale
        )
        value_grad = jnp.einsum(
            "hij,ihd->jhd",
            attn.astype(jnp.bfloat16),
            cotan_part,
            preferred_element_type=jnp.float32,
        )
        return (
            key_total + key_grad.reshape(row_count, feat_width),
            value_total + value_grad.reshape(row_count, feat_width),
        )

    zero_rows = jnp.zeros((row_count, feat_width), jnp.float32)
    zero_rab = jnp.zeros((head_count, bucket_total), jnp.float32)

    def tile_all(totals, tiles, info):
        tile_query, tile_key, tile_value, tile_cotan = tiles
        query_state = query_side((totals[0], totals[1]), tile_key, tile_value, info)
        key_state = key_side((totals[2], totals[3]), tile_query, tile_cotan, info)
        return (query_state[0], query_state[1], key_state[0], key_state[1])

    pieces = (
        lax.all_gather(queries, "ctx", axis=0, tiled=True),
        lax.all_gather(key_rows, "ctx", axis=0, tiled=True),
        lax.all_gather(value_rows, "ctx", axis=0, tiled=True),
        lax.all_gather(grad_out, "ctx", axis=0, tiled=True),
    )
    tile_count = pieces[0].shape[0] // row_count
    stacked = tuple((piece.reshape(tile_count, row_count, feat_width) for piece in pieces))

    def step(carry, item):
        tile_index = item[0]
        info = make_info(tile_index * row_count, row_count)
        return (tile_all(carry, item[1:], info), None)

    result, unused = lax.scan(
        step,
        (zero_rows, zero_rab, zero_rows, zero_rows),
        (jnp.arange(tile_count, dtype=jnp.int32),) + stacked,
    )
    totals = result
    query_total, rab_total, key_total, value_total = totals
    grad_rab = lax.psum(rab_total, ("dp", "ctx"))
    return (
        query_total.astype(jnp.bfloat16),
        key_total.astype(jnp.bfloat16),
        value_total.astype(jnp.bfloat16),
        grad_rab,
    )


def solution(mesh):
    if mesh.shape["ctx"] == 4:
        body = functools.partial(four_block_device, mesh.shape["dp"])
    else:
        body = scan_device
    return jax.shard_map(
        body,
        mesh=mesh,
        in_specs=(
            P(("dp", "ctx"), None),
            P(("dp", "ctx"), None),
            P(("dp", "ctx"), None),
            P(("dp", "ctx"), None),
            P(),
            P("dp", None),
            P("dp", None),
            P("dp", None),
        ),
        out_specs=(P(("dp", "ctx"), None), P(("dp", "ctx"), None), P(("dp", "ctx"), None), P()),
        check_vma=False,
    )
```

```python
import functools

import jax
import jax.numpy as jnp
from jax import lax
from jax.experimental import pallas as pl
from jax.experimental.pallas import tpu as pltpu
from jax.sharding import PartitionSpec as P

MESH = pl.DeviceIdType.MESH
F32 = jnp.float32
BF16 = jnp.bfloat16


def bucket_count(distance, bucket_total):
    value = distance + 1
    result = jnp.zeros(distance.shape, jnp.int32)
    for power in range(1, bucket_total):
        result = result + jnp.where(value >= 2**power, 1, 0).astype(jnp.int32)
    return result


def dot_nt(a, b):
    return lax.dot_general(a, b, (((1,), (1,)), ((), ())), preferred_element_type=F32)


def dot_nn(a, b):
    return lax.dot_general(a, b, (((1,), (0,)), ((), ())), preferred_element_type=F32)


def dot_tn(a, b):
    return lax.dot_general(a, b, (((0,), (0,)), ((), ())), preferred_element_type=F32)


def fused_kernel(
    n_dp,
    head_count,
    bucket_total,
    order_hbm,
    first_hbm,
    fill_hbm,
    q_hbm,
    k_hbm,
    v_hbm,
    d_hbm,
    table_hbm,
    gq_ref,
    gk_ref,
    gv_ref,
    rab_ref,
    order_ref,
    first_ref,
    fill_ref,
    q_ref,
    k_ref,
    vm,
    dm,
    table_ref,
    in_sems,
    send1,
    send2,
    base2,
    recv1,
    recv2,
    recv3,
    accq,
    acck,
    accv,
    biasv,
    rabs,
    ctx_slots,
    dp_slots,
    s1_send,
    s1_recv,
    s2_send,
    s2_recv,
    s3_send,
    s3_recv,
    rc_send,
    rc_recv,
    rd_send,
    rd_recv,
):
    rows = q_ref.shape[0]
    dim = q_ref.shape[1] // head_count
    scale = dim ** (-0.5)
    blocks = 4
    dp = lax.axis_index("dp")
    me = lax.axis_index("ctx")
    sib = me + 1 - 2 * (me % 2)
    cross = (me + 2) % 4
    diag = (sib + 2) % 4

    barrier = pltpu.get_barrier_semaphore()
    for step in range(1, blocks):
        pl.semaphore_signal(barrier, inc=1, device_id=(dp, (me + step) % blocks), device_id_type=MESH)
    for step in range(1, n_dp):
        pl.semaphore_signal(barrier, inc=1, device_id=((dp + step) % n_dp, me), device_id_type=MESH)

    fetches = [
        pltpu.make_async_copy(source, target, in_sems.at[index])
        for index, (source, target) in enumerate((
            (order_hbm, order_ref), (first_hbm, first_ref), (fill_hbm, fill_ref), (q_hbm, q_ref),
            (k_hbm, k_ref), (v_hbm, vm), (d_hbm, dm), (table_hbm, table_ref),
        ))
    ]
    for fetch in fetches:
        fetch.start()

    for fetch in fetches:
        fetch.wait()
    pl.semaphore_wait(barrier, blocks - 1 + n_dp - 1)

    last = blocks - 1
    log_me = order_ref[0, me]
    log_sib = order_ref[0, sib]
    log_cross = order_ref[0, cross]
    log_diag = order_ref[0, diag]
    hist_me = first_ref[0, log_me]
    fill_me = fill_ref[0, log_me]
    length = jnp.int32(0)
    for block in range(blocks):
        length = length + jnp.where(first_ref[0, block] == hist_me, fill_ref[0, block], 0)
    inverse = 1.0 / jnp.full((1, rows), length, jnp.int32).astype(F32)

    idle = log_me == last
    with_idle = idle | (log_sib == last)

    row_wide = lax.broadcasted_iota(jnp.int32, (rows, dim), 0)
    row_ok = jnp.where(row_wide < fill_me, 1.0, 0.0).astype(F32).astype(BF16)

    def cols(h):
        return pl.ds(pl.multiple_of(h * dim, dim), dim)

    log_one = jnp.where(log_sib == last, log_diag, log_sib)
    log_two = jnp.where(log_cross == last, log_diag, log_cross)
    early_one = log_me < log_one
    early_two = log_me < log_two

    def prepare(h):
        at = cols(h)
        q_h, k_h = q_ref[:, at], k_ref[:, at]
        v_h, d_h = vm[:, at] * row_ok, dm[:, at] * row_ok
        vm[:, at] = v_h
        dm[:, at] = d_h
        send1[h, 0] = jnp.where(early_one, k_h, q_h)
        send1[h, 1] = jnp.where(early_one, v_h, d_h)
        base2[h, 0] = jnp.where(early_two, k_h, q_h)
        base2[h, 1] = jnp.where(early_two, v_h, d_h)

    def copy1(h):
        return pltpu.make_async_remote_copy(
            src_ref=send1.at[h], dst_ref=recv1.at[h], send_sem=s1_send.at[h], recv_sem=s1_recv.at[h],
            device_id=(dp, sib), device_id_type=MESH)

    def copy2(h):
        return pltpu.make_async_remote_copy(
            src_ref=send2.at[h], dst_ref=recv2.at[h], send_sem=s2_send.at[h], recv_sem=s2_recv.at[h],
            device_id=(dp, cross), device_id_type=MESH)

    def copy3(h):
        return pltpu.make_async_remote_copy(
            src_ref=recv2.at[h], dst_ref=recv3.at[h], send_sem=s3_send.at[h], recv_sem=s3_recv.at[h],
            device_id=(dp, sib), device_id_type=MESH)

    def prepare_and_send(h, carry):
        prepare(h)
        copy1(h).start()
        return carry

    lax.fori_loop(0, head_count, prepare_and_send, 0)

    table = table_ref[...]
    lane = lax.broadcasted_iota(jnp.int32, (head_count, 2 * rows), 1)
    offset = jnp.where(lane < rows, -lane, 2 * rows - lane)

    def distance_of(delta):
        return jnp.abs(delta * rows + offset)

    log_a = jnp.where(with_idle, log_diag, log_sib)
    log_b = log_two
    delta_a, delta_b = log_me - log_a, log_me - log_b
    buckets = (
        bucket_count(jnp.maximum(offset, 0), bucket_total),
        bucket_count(distance_of(delta_a), bucket_total),
        bucket_count(distance_of(delta_b), bucket_total),
    )
    for kind in range(3):
        filled = jnp.zeros((head_count, 2 * rows), F32)
        for b in range(bucket_total):
            filled = jnp.where(buckets[kind] == b, table[:, b : b + 1], filled)
        for h in range(head_count):
            biasv[kind, h] = filled[h : h + 1] * 0.5

    for h in range(head_count):
        copy1(h).wait_recv()
        send2[h] = jnp.where(idle, recv1[h], base2[h])
        copy2(h).start()

    i_row = lax.broadcasted_iota(jnp.int32, (rows, rows), 0)
    j_col = lax.broadcasted_iota(jnp.int32, (rows, rows), 1)

    def bias_of(kind, h):
        spread = jnp.broadcast_to(biasv[kind, h], (rows, 2 * rows))
        return pltpu.roll(spread, 0, 1, stride=1, stride_axis=0)[:, :rows]

    lane8 = lax.broadcasted_iota(jnp.int32, (8, rows), 1)

    def by_offset(grad_score):
        low = jnp.zeros((8, rows), F32)
        high = jnp.zeros((8, rows), F32)
        for start in range(0, rows, 8):
            part = grad_score[start : start + 8, :]
            if start == 0:
                low = low + part
            else:
                turned = pltpu.roll(part, rows - start, 1)
                wrapped = lane8 >= rows - start
                low = low + jnp.where(wrapped, 0.0, turned)
                high = high + jnp.where(wrapped, turned, 0.0)
        return low, high

    def pair_terms(score_dot, grad_dot, bias, factor):
        half = score_dot * (scale * 0.5) + bias
        turn = jnp.tanh(half)
        up = 1.0 + turn
        raw = half * up
        attn = raw * factor
        slope = (up + raw * (1.0 - turn)) * (factor * 0.5)
        return attn.astype(BF16), grad_dot * slope

    def own_pair(h):
        at = cols(h)
        q_h, k_h, v_h, d_h = q_ref[:, at], k_ref[:, at], vm[:, at], dm[:, at]
        factor = jnp.where(j_col <= i_row, inverse, 0.0)
        attn, grad_score = pair_terms(dot_nt(q_h, k_h), dot_nt(d_h, v_h), bias_of(0, h), factor)
        low_score = grad_score.astype(BF16)
        accq[h] = dot_nn(low_score, k_h)
        acck[h] = dot_tn(low_score, q_h)
        accv[h] = dot_tn(attn, d_h)
        low, high = by_offset(grad_score)
        rabs[0, h, :, :rows] = low
        rabs[0, h, :, rows:] = high

    def other_pair(kind, h, part0, part1, delta, factor):
        at = cols(h)
        later = delta > 0
        own0 = jnp.where(later, q_ref[:, at], k_ref[:, at])
        own1 = jnp.where(later, dm[:, at], vm[:, at])
        attn, grad_score = pair_terms(dot_nt(own0, part0), dot_nt(own1, part1), bias_of(kind, h), factor)
        term0 = dot_nn(grad_score.astype(BF16), part0)
        term1 = dot_nn(attn, part1)
        low, high = by_offset(grad_score)
        take = jnp.where(later, 1.0, 0.0)
        rabs[kind, h, :, :rows] = low * take
        rabs[kind, h, :, rows:] = high * take
        return jnp.where(later, term0, 0.0), jnp.where(later, 0.0, term0), jnp.where(later, 0.0, term1)

    factor_a = jnp.where(first_ref[0, log_a] == hist_me, inverse, 0.0)
    factor_b = jnp.where(first_ref[0, log_b] == hist_me, inverse, 0.0)
    factor_a = jnp.where(idle, 0.0, factor_a)
    factor_b = jnp.where(idle, 0.0, factor_b)

    def own_step(h, carry):
        own_pair(h)
        return carry

    lax.fori_loop(0, head_count, own_step, 0)

    def other_step(h, carry):
        at = cols(h)
        copy2(h).wait_recv()
        copy3(h).start()
        q_b, k_b, v_b = other_pair(2, h, recv2[h, 0], recv2[h, 1], delta_b, factor_b)
        copy3(h).wait_recv()
        part0 = jnp.where(with_idle, recv3[h, 0], recv1[h, 0])
        part1 = jnp.where(with_idle, recv3[h, 1], recv1[h, 1])
        q_a, k_a, v_a = other_pair(1, h, part0, part1, delta_a, factor_a)
        ok = row_wide < fill_me
        gq_ref[:, at] = ((accq[h] + q_a + q_b) * scale).astype(BF16)
        gk_ref[:, at] = ((acck[h] + k_a + k_b) * scale).astype(BF16)
        gv_ref[:, at] = jnp.where(ok, accv[h] + v_a + v_b, 0.0).astype(BF16)
        return carry

    lax.fori_loop(0, head_count, other_step, 0)

    lane_out = lax.broadcasted_iota(jnp.int32, (head_count, 128), 1)
    lane_sum = lax.broadcasted_iota(jnp.int32, (8, 2 * rows), 1)
    offset_sum = lax.broadcasted_iota(jnp.int32, (8, 2 * rows), 0) - jnp.where(
        lane_sum < rows, lane_sum, lane_sum - 2 * rows
    )
    sum_buckets = (
        bucket_count(jnp.maximum(offset_sum, 0), bucket_total),
        bucket_count(jnp.abs(delta_a * rows + offset_sum), bucket_total),
        bucket_count(jnp.abs(delta_b * rows + offset_sum), bucket_total),
    )
    mine = jnp.zeros((head_count, 128), F32)
    for b in range(bucket_total):
        here = [sum_buckets[kind] == b for kind in range(3)]
        per_head = []
        for h in range(head_count):
            picked = jnp.zeros((8, 2 * rows), F32)
            for kind in range(3):
                picked = picked + jnp.where(here[kind], rabs[kind, h], 0.0)
            per_head.append(jnp.sum(picked, axis=0, keepdims=True))
        sums = jnp.sum(jnp.concatenate(per_head, axis=0), axis=1, keepdims=True)
        mine = jnp.where(lane_out == b, sums, mine)
    ctx_slots[me] = jnp.concatenate([mine, jnp.zeros((8 - head_count, 128), F32)], axis=0)

    def rab_ctx(step, owner):
        return pltpu.make_async_remote_copy(
            src_ref=ctx_slots.at[owner], dst_ref=ctx_slots.at[owner], send_sem=rc_send.at[step],
            recv_sem=rc_recv.at[owner], device_id=(dp, (me + step) % blocks), device_id_type=MESH)

    def rab_dp(step, owner):
        return pltpu.make_async_remote_copy(
            src_ref=dp_slots.at[owner], dst_ref=dp_slots.at[owner], send_sem=rd_send.at[step],
            recv_sem=rd_recv.at[owner], device_id=((dp + step) % n_dp, me), device_id_type=MESH)

    for step in range(1, blocks):
        rab_ctx(step, me).start()
    for step in range(1, blocks):
        rab_ctx(step, (me + step) % blocks).wait_recv()
    total = ctx_slots[0]
    for slot in range(1, blocks):
        total = total + ctx_slots[slot]
    dp_slots[dp] = total
    for step in range(1, n_dp):
        rab_dp(step, dp).start()
    for h in range(head_count):
        copy1(h).wait_send()
        copy2(h).wait_send()
        copy3(h).wait_send()
    for step in range(1, blocks):
        rab_ctx(step, me).wait_send()
    for step in range(1, n_dp):
        rab_dp(step, (dp + step) % n_dp).wait_recv()
    total = dp_slots[0]
    for slot in range(1, n_dp):
        total = total + dp_slots[slot]
    for step in range(1, n_dp):
        rab_dp(step, dp).wait_send()
    rab_ref[...] = total[:head_count, :bucket_total]


def hand_over(*refs):
    sources, targets, held, in_sems, out_sems = refs[:4], refs[4:8], refs[8:12], refs[12], refs[13]
    loads = [pltpu.make_async_copy(sources[i], held[i], in_sems.at[i]) for i in range(4)]
    stores = [pltpu.make_async_copy(held[i], targets[i], out_sems.at[i]) for i in range(4)]
    for load in loads:
        load.start()
    for load, store in zip(loads, stores):
        load.wait()
        store.start()
    for store in stores:
        store.wait()


def four_block_device(
    n_dp, queries, key_rows, value_rows, grad_out, rab_table, first_block, block_fill, block_order
):
    rows, width = queries.shape
    heads, bucket_total = rab_table.shape
    dim = width // heads
    vmem = pl.BlockSpec(memory_space=pltpu.VMEM)
    out = jax.ShapeDtypeStruct((rows, width), BF16)
    buf = pltpu.VMEM((heads, 2, rows, dim), BF16)
    acc = pltpu.VMEM((heads, rows, dim), F32)
    dma = pltpu.SemaphoreType.DMA
    outs = pl.pallas_call(
        functools.partial(fused_kernel, n_dp, heads, bucket_total),
        out_shape=(out, out, out, jax.ShapeDtypeStruct((heads, bucket_total), F32)),
        in_specs=[pl.BlockSpec(memory_space=pltpu.HBM)] * 8,
        out_specs=(vmem,) * 4,
        scratch_shapes=[
            pltpu.SMEM(block_order.shape, jnp.int32),
            pltpu.SMEM(first_block.shape, jnp.int32),
            pltpu.SMEM(block_fill.shape, jnp.int32),
            pltpu.VMEM((rows, width), BF16),
            pltpu.VMEM((rows, width), BF16),
            pltpu.VMEM((rows, width), BF16),
            pltpu.VMEM((rows, width), BF16),
            pltpu.VMEM(rab_table.shape, F32),
            dma((8,)),
            buf, buf, buf, buf, buf, buf,
            acc, acc, acc,
            pltpu.VMEM((3, heads, 1, 2 * rows), F32),
            pltpu.VMEM((3, heads, 8, 2 * rows), F32),
            pltpu.VMEM((4, 8, 128), F32),
            pltpu.VMEM((n_dp, 8, 128), F32),
            dma((heads,)), dma((heads,)), dma((heads,)), dma((heads,)), dma((heads,)), dma((heads,)),
            dma((4,)), dma((4,)), dma((n_dp,)), dma((n_dp,)),
        ],
        compiler_params=pltpu.CompilerParams(
            collective_id=0, has_side_effects=True
        ),
    )(block_order, first_block, block_fill, queries, key_rows, value_rows, grad_out, rab_table)
    hbm = pl.BlockSpec(memory_space=pltpu.HBM)
    return pl.pallas_call(
        hand_over,
        out_shape=tuple(jax.ShapeDtypeStruct(one.shape, one.dtype) for one in outs),
        in_specs=[hbm] * 4,
        out_specs=(hbm,) * 4,
        scratch_shapes=[pltpu.VMEM(one.shape, one.dtype) for one in outs] + [dma((4,)), dma((4,))],
    )(*outs)


def bucket_of(distance, bucket_total):
    value = distance + 1
    guess = jnp.floor(jnp.log2(value.astype(jnp.float32))).astype(jnp.int32)
    guess = jnp.clip(guess, 0, 29)
    guess = guess - (jnp.left_shift(jnp.ones_like(guess), guess) > value).astype(jnp.int32)
    guess = guess + (jnp.left_shift(jnp.ones_like(guess), guess + 1) <= value).astype(jnp.int32)
    return jnp.clip(guess, 0, bucket_total - 1)


def lookup(table, index_rows, table_len):
    chosen = (index_rows[:, None] == jnp.arange(table_len, dtype=jnp.int32)[None, :]).astype(
        jnp.int32
    )
    return jnp.sum(chosen * table[None, :], axis=1)


def live_of(query_info, key_info):
    query_pos, query_hist, query_valid, query_inv = query_info
    key_pos, key_hist, key_valid, key_inv = key_info
    live_mask = (query_hist[:, None] == key_hist[None, :]) & (
        key_pos[None, :] <= query_pos[:, None]
    )
    return live_mask & query_valid[:, None] & key_valid[None, :]


def pair_core(
    query_part, key_part, value_part, cotan_part, query_info, key_info, rab_table, score_scale
):
    live_f = live_of(query_info, key_info).astype(jnp.float32)
    query_inv = query_info[3]
    bucket = bucket_of(
        jnp.maximum(query_info[0][:, None] - key_info[0][None, :], 0), rab_table.shape[1]
    )
    score_bias = jnp.take(rab_table, bucket, axis=1)
    scores = (
        jnp.einsum("ihd,jhd->hij", query_part, key_part, preferred_element_type=jnp.float32)
        * score_scale
        + score_bias
    )
    sigmoid_s = jax.nn.sigmoid(scores)
    attn = scores * sigmoid_s * live_f * query_inv[None, :, None]
    grad_attn = (
        jnp.einsum("ihd,jhd->hij", cotan_part, value_part, preferred_element_type=jnp.float32)
        * live_f
        * query_inv[None, :, None]
    )
    grad_score = grad_attn * (sigmoid_s * (1.0 + scores * (1.0 - sigmoid_s)))
    return (attn, grad_score, bucket)


def bias_terms(grad_score, bucket, bucket_total):
    one_hot = (
        bucket.reshape(-1)[:, None] == jnp.arange(bucket_total, dtype=jnp.int32)[None, :]
    ).astype(jnp.float32)
    flat_grad = grad_score.reshape(grad_score.shape[0], -1)
    return jnp.dot(
        flat_grad, one_hot, precision=lax.Precision.HIGHEST, preferred_element_type=jnp.float32
    )


def scan_device(
    queries, key_rows, value_rows, grad_out, rab_table, first_block, block_fill, block_order
):
    row_count, feat_width = queries.shape
    head_count, bucket_total = rab_table.shape
    head_dim = feat_width // head_count
    score_scale = head_dim ** (-0.5)
    block_total = first_block.shape[1]
    head_block = first_block[0]
    fill_count = block_fill[0]
    slot_order = block_order[0]
    same_hist = (head_block[:, None] == head_block[None, :]).astype(jnp.int32)
    hist_len = jnp.sum(same_hist * fill_count[None, :], axis=1)
    slot_hist = lookup(head_block, slot_order, block_total)
    slot_fill = lookup(fill_count, slot_order, block_total)
    slot_len = lookup(hist_len, slot_order, block_total)

    def make_info(offset, count_rows):
        row_ids = offset + jnp.arange(count_rows, dtype=jnp.int32)
        slot_ids = row_ids // row_count
        within = row_ids - slot_ids * row_count
        logical = lookup(slot_order, slot_ids, block_total)
        positions = logical * row_count + within
        hist_ids = lookup(slot_hist, slot_ids, block_total)
        valid_rows = within < lookup(slot_fill, slot_ids, block_total)
        inverse_len = 1.0 / lookup(slot_len, slot_ids, block_total).astype(jnp.float32)
        return (positions, hist_ids, valid_rows, inverse_len)

    own_info = make_info(lax.axis_index("ctx") * row_count, row_count)
    own_query = queries.reshape(row_count, head_count, head_dim)
    own_key = key_rows.reshape(row_count, head_count, head_dim)
    own_value = value_rows.reshape(row_count, head_count, head_dim)
    own_cotan = grad_out.reshape(row_count, head_count, head_dim)

    def query_side(state, piece_key, piece_value, info):
        count_rows = piece_key.shape[0]
        key_part = piece_key.reshape(count_rows, head_count, head_dim)
        value_part = piece_value.reshape(count_rows, head_count, head_dim)
        query_total, rab_total = state
        attn, grad_score, bucket = pair_core(
            own_query, key_part, value_part, own_cotan, own_info, info, rab_table, score_scale
        )
        score_low = grad_score.astype(jnp.bfloat16)
        query_grad = (
            jnp.einsum("hij,jhd->ihd", score_low, key_part, preferred_element_type=jnp.float32)
            * score_scale
        )
        rab_terms = bias_terms(grad_score, bucket, bucket_total)
        return (query_total + query_grad.reshape(row_count, feat_width), rab_total + rab_terms)

    def key_side(state, piece_query, piece_cotan, info):
        count_rows = piece_query.shape[0]
        query_part = piece_query.reshape(count_rows, head_count, head_dim)
        cotan_part = piece_cotan.reshape(count_rows, head_count, head_dim)
        key_total, value_total = state
        attn, grad_score, bucket = pair_core(
            query_part, own_key, own_value, cotan_part, info, own_info, rab_table, score_scale
        )
        key_grad = (
            jnp.einsum(
                "hij,ihd->jhd",
                grad_score.astype(jnp.bfloat16),
                query_part,
                preferred_element_type=jnp.float32,
            )
            * score_scale
        )
        value_grad = jnp.einsum(
            "hij,ihd->jhd",
            attn.astype(jnp.bfloat16),
            cotan_part,
            preferred_element_type=jnp.float32,
        )
        return (
            key_total + key_grad.reshape(row_count, feat_width),
            value_total + value_grad.reshape(row_count, feat_width),
        )

    zero_rows = jnp.zeros((row_count, feat_width), jnp.float32)
    zero_rab = jnp.zeros((head_count, bucket_total), jnp.float32)

    def tile_all(totals, tiles, info):
        tile_query, tile_key, tile_value, tile_cotan = tiles
        query_state = query_side((totals[0], totals[1]), tile_key, tile_value, info)
        key_state = key_side((totals[2], totals[3]), tile_query, tile_cotan, info)
        return (query_state[0], query_state[1], key_state[0], key_state[1])

    pieces = (
        lax.all_gather(queries, "ctx", axis=0, tiled=True),
        lax.all_gather(key_rows, "ctx", axis=0, tiled=True),
        lax.all_gather(value_rows, "ctx", axis=0, tiled=True),
        lax.all_gather(grad_out, "ctx", axis=0, tiled=True),
    )
    tile_count = pieces[0].shape[0] // row_count
    stacked = tuple((piece.reshape(tile_count, row_count, feat_width) for piece in pieces))

    def step(carry, item):
        tile_index = item[0]
        info = make_info(tile_index * row_count, row_count)
        return (tile_all(carry, item[1:], info), None)

    result, unused = lax.scan(
        step,
        (zero_rows, zero_rab, zero_rows, zero_rows),
        (jnp.arange(tile_count, dtype=jnp.int32),) + stacked,
    )
    totals = result
    query_total, rab_total, key_total, value_total = totals
    grad_rab = lax.psum(rab_total, ("dp", "ctx"))
    return (
        query_total.astype(jnp.bfloat16),
        key_total.astype(jnp.bfloat16),
        value_total.astype(jnp.bfloat16),
        grad_rab,
    )


def solution(mesh):
    if mesh.shape["ctx"] == 4:
        body = functools.partial(four_block_device, mesh.shape["dp"])
    else:
        body = scan_device
    return jax.shard_map(
        body,
        mesh=mesh,
        in_specs=(
            P(("dp", "ctx"), None),
            P(("dp", "ctx"), None),
            P(("dp", "ctx"), None),
            P(("dp", "ctx"), None),
            P(),
            P("dp", None),
            P("dp", None),
            P("dp", None),
        ),
        out_specs=(P(("dp", "ctx"), None), P(("dp", "ctx"), None), P(("dp", "ctx"), None), P()),
        check_vma=False,
    )
```

```python
import functools

import jax
import jax.numpy as jnp
from jax import lax
from jax.experimental import pallas as pl
from jax.experimental.pallas import tpu as pltpu
from jax.sharding import PartitionSpec as P

MESH = pl.DeviceIdType.MESH
F32 = jnp.float32
BF16 = jnp.bfloat16


def bucket_count(distance, bucket_total):
    value = distance + 1
    result = jnp.zeros(distance.shape, jnp.int32)
    for power in range(1, bucket_total):
        result = result + jnp.where(value >= 2**power, 1, 0).astype(jnp.int32)
    return result


def dot_nt(a, b):
    return lax.dot_general(a, b, (((1,), (1,)), ((), ())), preferred_element_type=F32)


def dot_nn(a, b):
    return lax.dot_general(a, b, (((1,), (0,)), ((), ())), preferred_element_type=F32)


def dot_tn(a, b):
    return lax.dot_general(a, b, (((0,), (0,)), ((), ())), preferred_element_type=F32)


def fused_kernel(
    n_dp,
    head_count,
    bucket_total,
    order_hbm,
    first_hbm,
    fill_hbm,
    q_hbm,
    k_hbm,
    v_hbm,
    d_hbm,
    table_hbm,
    gq_ref,
    gk_ref,
    gv_ref,
    rab_ref,
    order_ref,
    first_ref,
    fill_ref,
    q_ref,
    k_ref,
    vm,
    dm,
    table_ref,
    in_sems,
    send1,
    send2,
    base2,
    recv1,
    recv2,
    recv3,
    accq,
    acck,
    accv,
    biasv,
    rabs,
    rab_rows,
    ctx_slots,
    dp_slots,
    s1_send,
    s1_recv,
    s2_send,
    s2_recv,
    s3_send,
    s3_recv,
    rc_send,
    rc_recv,
    rd_send,
    rd_recv,
):
    rows = q_ref.shape[0]
    dim = q_ref.shape[1] // head_count
    scale = dim ** (-0.5)
    blocks = 4
    dp = lax.axis_index("dp")
    me = lax.axis_index("ctx")
    sib = me + 1 - 2 * (me % 2)
    cross = (me + 2) % 4
    diag = (sib + 2) % 4

    barrier = pltpu.get_barrier_semaphore()
    for step in range(1, blocks):
        pl.semaphore_signal(barrier, inc=1, device_id=(dp, (me + step) % blocks), device_id_type=MESH)
    for step in range(1, n_dp):
        pl.semaphore_signal(barrier, inc=1, device_id=((dp + step) % n_dp, me), device_id_type=MESH)

    fetches = [
        pltpu.make_async_copy(source, target, in_sems.at[index])
        for index, (source, target) in enumerate((
            (order_hbm, order_ref), (first_hbm, first_ref), (fill_hbm, fill_ref), (q_hbm, q_ref),
            (k_hbm, k_ref), (v_hbm, vm), (d_hbm, dm), (table_hbm, table_ref),
        ))
    ]
    for fetch in fetches:
        fetch.start()

    for fetch in fetches:
        fetch.wait()
    pl.semaphore_wait(barrier, blocks - 1 + n_dp - 1)

    last = blocks - 1
    log_me = order_ref[0, me]
    log_sib = order_ref[0, sib]
    log_cross = order_ref[0, cross]
    log_diag = order_ref[0, diag]
    hist_me = first_ref[0, log_me]
    fill_me = fill_ref[0, log_me]
    length = jnp.int32(0)
    for block in range(blocks):
        length = length + jnp.where(first_ref[0, block] == hist_me, fill_ref[0, block], 0)
    inverse = 1.0 / jnp.full((1, rows), length, jnp.int32).astype(F32)

    idle = log_me == last
    with_idle = idle | (log_sib == last)

    row_wide = lax.broadcasted_iota(jnp.int32, (rows, dim), 0)
    row_ok = jnp.where(row_wide < fill_me, 1.0, 0.0).astype(F32).astype(BF16)

    def cols(h):
        return pl.ds(pl.multiple_of(h * dim, dim), dim)

    log_one = jnp.where(log_sib == last, log_diag, log_sib)
    log_two = jnp.where(log_cross == last, log_diag, log_cross)
    early_one = log_me < log_one
    early_two = log_me < log_two

    def prepare(h):
        at = cols(h)
        q_h, k_h = q_ref[:, at], k_ref[:, at]
        v_h, d_h = vm[:, at] * row_ok, dm[:, at] * row_ok
        vm[:, at] = v_h
        dm[:, at] = d_h
        send1[h, 0] = jnp.where(early_one, k_h, q_h)
        send1[h, 1] = jnp.where(early_one, v_h, d_h)
        base2[h, 0] = jnp.where(early_two, k_h, q_h)
        base2[h, 1] = jnp.where(early_two, v_h, d_h)

    def copy1(h):
        return pltpu.make_async_remote_copy(
            src_ref=send1.at[h], dst_ref=recv1.at[h], send_sem=s1_send.at[h], recv_sem=s1_recv.at[h],
            device_id=(dp, sib), device_id_type=MESH)

    def copy2(h):
        return pltpu.make_async_remote_copy(
            src_ref=send2.at[h], dst_ref=recv2.at[h], send_sem=s2_send.at[h], recv_sem=s2_recv.at[h],
            device_id=(dp, cross), device_id_type=MESH)

    def copy3(h):
        return pltpu.make_async_remote_copy(
            src_ref=recv2.at[h], dst_ref=recv3.at[h], send_sem=s3_send.at[h], recv_sem=s3_recv.at[h],
            device_id=(dp, sib), device_id_type=MESH)

    def prepare_and_send(h, carry):
        prepare(h)
        copy1(h).start()
        return carry

    lax.fori_loop(0, head_count, prepare_and_send, 0)

    table = table_ref[...]
    lane = lax.broadcasted_iota(jnp.int32, (head_count, 2 * rows), 1)
    offset = jnp.where(lane < rows, -lane, 2 * rows - lane)

    def distance_of(delta):
        return jnp.abs(delta * rows + offset)

    log_a = jnp.where(with_idle, log_diag, log_sib)
    log_b = log_two
    delta_a, delta_b = log_me - log_a, log_me - log_b
    buckets = (
        bucket_count(jnp.maximum(offset, 0), bucket_total),
        bucket_count(distance_of(delta_a), bucket_total),
        bucket_count(distance_of(delta_b), bucket_total),
    )
    for kind in range(3):
        filled = jnp.zeros((head_count, 2 * rows), F32)
        for b in range(bucket_total):
            filled = jnp.where(buckets[kind] == b, table[:, b : b + 1], filled)
        for h in range(head_count):
            biasv[kind, h] = filled[h : h + 1] * 0.5

    for h in range(head_count):
        copy1(h).wait_recv()
        send2[h] = jnp.where(idle, recv1[h], base2[h])
        copy2(h).start()

    i_row = lax.broadcasted_iota(jnp.int32, (rows, rows), 0)
    j_col = lax.broadcasted_iota(jnp.int32, (rows, rows), 1)

    def bias_of(kind, h):
        spread = jnp.broadcast_to(biasv[kind, h], (rows, 2 * rows))
        return pltpu.roll(spread, 0, 1, stride=1, stride_axis=0)[:, :rows]

    lane8 = lax.broadcasted_iota(jnp.int32, (8, rows), 1)

    def by_offset(grad_score):
        low = jnp.zeros((8, rows), F32)
        high = jnp.zeros((8, rows), F32)
        for start in range(0, rows, 8):
            part = grad_score[start : start + 8, :]
            if start == 0:
                low = low + part
            else:
                turned = pltpu.roll(part, rows - start, 1)
                wrapped = lane8 >= rows - start
                low = low + jnp.where(wrapped, 0.0, turned)
                high = high + jnp.where(wrapped, turned, 0.0)
        return low, high

    def pair_terms(score_dot, grad_dot, bias, factor):
        half = score_dot * (scale * 0.5) + bias
        turn = jnp.tanh(half)
        up = 1.0 + turn
        raw = half * up
        attn = raw * factor
        slope = (up + raw * (1.0 - turn)) * (factor * 0.5)
        return attn.astype(BF16), grad_dot * slope

    def own_pair(h):
        at = cols(h)
        q_h, k_h, v_h, d_h = q_ref[:, at], k_ref[:, at], vm[:, at], dm[:, at]
        factor = jnp.where(j_col <= i_row, inverse, 0.0)
        attn, grad_score = pair_terms(dot_nt(q_h, k_h), dot_nt(d_h, v_h), bias_of(0, h), factor)
        low_score = grad_score.astype(BF16)
        accq[h] = dot_nn(low_score, k_h)
        acck[h] = dot_tn(low_score, q_h)
        accv[h] = dot_tn(attn, d_h)
        low, high = by_offset(grad_score)
        rabs[0, h, :, :rows] = low
        rabs[0, h, :, rows:] = high

    def other_pair(kind, h, part0, part1, delta, factor):
        at = cols(h)
        later = delta > 0
        own0 = jnp.where(later, q_ref[:, at], k_ref[:, at])
        own1 = jnp.where(later, dm[:, at], vm[:, at])
        attn, grad_score = pair_terms(dot_nt(own0, part0), dot_nt(own1, part1), bias_of(kind, h), factor)
        term0 = dot_nn(grad_score.astype(BF16), part0)
        term1 = dot_nn(attn, part1)
        low, high = by_offset(grad_score)
        take = jnp.where(later, 1.0, 0.0)
        rabs[kind, h, :, :rows] = low * take
        rabs[kind, h, :, rows:] = high * take
        return jnp.where(later, term0, 0.0), jnp.where(later, 0.0, term0), jnp.where(later, 0.0, term1)

    factor_a = jnp.where(first_ref[0, log_a] == hist_me, inverse, 0.0)
    factor_b = jnp.where(first_ref[0, log_b] == hist_me, inverse, 0.0)
    factor_a = jnp.where(idle, 0.0, factor_a)
    factor_b = jnp.where(idle, 0.0, factor_b)

    def own_step(h, carry):
        own_pair(h)
        return carry

    lax.fori_loop(0, head_count, own_step, 0)

    lane_sum = lax.broadcasted_iota(jnp.int32, (8, 2 * rows), 1)
    offset_sum = lax.broadcasted_iota(jnp.int32, (8, 2 * rows), 0) - jnp.where(
        lane_sum < rows, lane_sum, lane_sum - 2 * rows
    )
    sum_buckets = (
        bucket_count(jnp.maximum(offset_sum, 0), bucket_total),
        bucket_count(jnp.abs(delta_a * rows + offset_sum), bucket_total),
        bucket_count(jnp.abs(delta_b * rows + offset_sum), bucket_total),
    )
    lane_out = lax.broadcasted_iota(jnp.int32, (1, 128), 1)

    def other_step(h, carry):
        at = cols(h)
        copy2(h).wait_recv()
        copy3(h).start()
        q_b, k_b, v_b = other_pair(2, h, recv2[h, 0], recv2[h, 1], delta_b, factor_b)
        copy3(h).wait_recv()
        part0 = jnp.where(with_idle, recv3[h, 0], recv1[h, 0])
        part1 = jnp.where(with_idle, recv3[h, 1], recv1[h, 1])
        q_a, k_a, v_a = other_pair(1, h, part0, part1, delta_a, factor_a)
        ok = row_wide < fill_me
        gq_ref[:, at] = ((accq[h] + q_a + q_b) * scale).astype(BF16)
        gk_ref[:, at] = ((acck[h] + k_a + k_b) * scale).astype(BF16)
        gv_ref[:, at] = jnp.where(ok, accv[h] + v_a + v_b, 0.0).astype(BF16)
        row = jnp.zeros((1, 128), F32)
        for b in range(bucket_total):
            picked = jnp.zeros((8, 2 * rows), F32)
            for kind in range(3):
                picked = picked + jnp.where(sum_buckets[kind] == b, rabs[kind, h], 0.0)
            folded = jnp.sum(picked, axis=0, keepdims=True)
            row = jnp.where(lane_out == b, jnp.sum(folded, axis=1, keepdims=True), row)
        rab_rows[h] = row
        return carry

    lax.fori_loop(0, head_count, other_step, 0)

    mine = jnp.concatenate([rab_rows[h] for h in range(head_count)], axis=0)
    ctx_slots[me] = jnp.concatenate([mine, jnp.zeros((8 - head_count, 128), F32)], axis=0)

    def rab_ctx(step, owner):
        return pltpu.make_async_remote_copy(
            src_ref=ctx_slots.at[owner], dst_ref=ctx_slots.at[owner], send_sem=rc_send.at[step],
            recv_sem=rc_recv.at[owner], device_id=(dp, (me + step) % blocks), device_id_type=MESH)

    def rab_dp(step, owner):
        return pltpu.make_async_remote_copy(
            src_ref=dp_slots.at[owner], dst_ref=dp_slots.at[owner], send_sem=rd_send.at[step],
            recv_sem=rd_recv.at[owner], device_id=((dp + step) % n_dp, me), device_id_type=MESH)

    for step in range(1, blocks):
        rab_ctx(step, me).start()
    for step in range(1, blocks):
        rab_ctx(step, (me + step) % blocks).wait_recv()
    total = ctx_slots[0]
    for slot in range(1, blocks):
        total = total + ctx_slots[slot]
    dp_slots[dp] = total
    for step in range(1, n_dp):
        rab_dp(step, dp).start()
    for h in range(head_count):
        copy1(h).wait_send()
        copy2(h).wait_send()
        copy3(h).wait_send()
    for step in range(1, blocks):
        rab_ctx(step, me).wait_send()
    for step in range(1, n_dp):
        rab_dp(step, (dp + step) % n_dp).wait_recv()
    total = dp_slots[0]
    for slot in range(1, n_dp):
        total = total + dp_slots[slot]
    for step in range(1, n_dp):
        rab_dp(step, dp).wait_send()
    rab_ref[...] = total[:head_count, :bucket_total]


def hand_over(*refs):
    sources, targets, held, in_sems, out_sems = refs[:4], refs[4:8], refs[8:12], refs[12], refs[13]
    loads = [pltpu.make_async_copy(sources[i], held[i], in_sems.at[i]) for i in range(4)]
    stores = [pltpu.make_async_copy(held[i], targets[i], out_sems.at[i]) for i in range(4)]
    for load in loads:
        load.start()
    for load, store in zip(loads, stores):
        load.wait()
        store.start()
    for store in stores:
        store.wait()


def four_block_device(
    n_dp, queries, key_rows, value_rows, grad_out, rab_table, first_block, block_fill, block_order
):
    rows, width = queries.shape
    heads, bucket_total = rab_table.shape
    dim = width // heads
    vmem = pl.BlockSpec(memory_space=pltpu.VMEM)
    out = jax.ShapeDtypeStruct((rows, width), BF16)
    buf = pltpu.VMEM((heads, 2, rows, dim), BF16)
    acc = pltpu.VMEM((heads, rows, dim), F32)
    dma = pltpu.SemaphoreType.DMA
    outs = pl.pallas_call(
        functools.partial(fused_kernel, n_dp, heads, bucket_total),
        out_shape=(out, out, out, jax.ShapeDtypeStruct((heads, bucket_total), F32)),
        in_specs=[pl.BlockSpec(memory_space=pltpu.HBM)] * 8,
        out_specs=(vmem,) * 4,
        scratch_shapes=[
            pltpu.SMEM(block_order.shape, jnp.int32),
            pltpu.SMEM(first_block.shape, jnp.int32),
            pltpu.SMEM(block_fill.shape, jnp.int32),
            pltpu.VMEM((rows, width), BF16),
            pltpu.VMEM((rows, width), BF16),
            pltpu.VMEM((rows, width), BF16),
            pltpu.VMEM((rows, width), BF16),
            pltpu.VMEM(rab_table.shape, F32),
            dma((8,)),
            buf, buf, buf, buf, buf, buf,
            acc, acc, acc,
            pltpu.VMEM((3, heads, 1, 2 * rows), F32),
            pltpu.VMEM((3, heads, 8, 2 * rows), F32),
            pltpu.VMEM((heads, 1, 128), F32),
            pltpu.VMEM((4, 8, 128), F32),
            pltpu.VMEM((n_dp, 8, 128), F32),
            dma((heads,)), dma((heads,)), dma((heads,)), dma((heads,)), dma((heads,)), dma((heads,)),
            dma((4,)), dma((4,)), dma((n_dp,)), dma((n_dp,)),
        ],
        compiler_params=pltpu.CompilerParams(
            collective_id=0, has_side_effects=True
        ),
    )(block_order, first_block, block_fill, queries, key_rows, value_rows, grad_out, rab_table)
    hbm = pl.BlockSpec(memory_space=pltpu.HBM)
    return pl.pallas_call(
        hand_over,
        out_shape=tuple(jax.ShapeDtypeStruct(one.shape, one.dtype) for one in outs),
        in_specs=[hbm] * 4,
        out_specs=(hbm,) * 4,
        scratch_shapes=[pltpu.VMEM(one.shape, one.dtype) for one in outs] + [dma((4,)), dma((4,))],
    )(*outs)


def bucket_of(distance, bucket_total):
    value = distance + 1
    guess = jnp.floor(jnp.log2(value.astype(jnp.float32))).astype(jnp.int32)
    guess = jnp.clip(guess, 0, 29)
    guess = guess - (jnp.left_shift(jnp.ones_like(guess), guess) > value).astype(jnp.int32)
    guess = guess + (jnp.left_shift(jnp.ones_like(guess), guess + 1) <= value).astype(jnp.int32)
    return jnp.clip(guess, 0, bucket_total - 1)


def lookup(table, index_rows, table_len):
    chosen = (index_rows[:, None] == jnp.arange(table_len, dtype=jnp.int32)[None, :]).astype(
        jnp.int32
    )
    return jnp.sum(chosen * table[None, :], axis=1)


def live_of(query_info, key_info):
    query_pos, query_hist, query_valid, query_inv = query_info
    key_pos, key_hist, key_valid, key_inv = key_info
    live_mask = (query_hist[:, None] == key_hist[None, :]) & (
        key_pos[None, :] <= query_pos[:, None]
    )
    return live_mask & query_valid[:, None] & key_valid[None, :]


def pair_core(
    query_part, key_part, value_part, cotan_part, query_info, key_info, rab_table, score_scale
):
    live_f = live_of(query_info, key_info).astype(jnp.float32)
    query_inv = query_info[3]
    bucket = bucket_of(
        jnp.maximum(query_info[0][:, None] - key_info[0][None, :], 0), rab_table.shape[1]
    )
    score_bias = jnp.take(rab_table, bucket, axis=1)
    scores = (
        jnp.einsum("ihd,jhd->hij", query_part, key_part, preferred_element_type=jnp.float32)
        * score_scale
        + score_bias
    )
    sigmoid_s = jax.nn.sigmoid(scores)
    attn = scores * sigmoid_s * live_f * query_inv[None, :, None]
    grad_attn = (
        jnp.einsum("ihd,jhd->hij", cotan_part, value_part, preferred_element_type=jnp.float32)
        * live_f
        * query_inv[None, :, None]
    )
    grad_score = grad_attn * (sigmoid_s * (1.0 + scores * (1.0 - sigmoid_s)))
    return (attn, grad_score, bucket)


def bias_terms(grad_score, bucket, bucket_total):
    one_hot = (
        bucket.reshape(-1)[:, None] == jnp.arange(bucket_total, dtype=jnp.int32)[None, :]
    ).astype(jnp.float32)
    flat_grad = grad_score.reshape(grad_score.shape[0], -1)
    return jnp.dot(
        flat_grad, one_hot, precision=lax.Precision.HIGHEST, preferred_element_type=jnp.float32
    )


def scan_device(
    queries, key_rows, value_rows, grad_out, rab_table, first_block, block_fill, block_order
):
    row_count, feat_width = queries.shape
    head_count, bucket_total = rab_table.shape
    head_dim = feat_width // head_count
    score_scale = head_dim ** (-0.5)
    block_total = first_block.shape[1]
    head_block = first_block[0]
    fill_count = block_fill[0]
    slot_order = block_order[0]
    same_hist = (head_block[:, None] == head_block[None, :]).astype(jnp.int32)
    hist_len = jnp.sum(same_hist * fill_count[None, :], axis=1)
    slot_hist = lookup(head_block, slot_order, block_total)
    slot_fill = lookup(fill_count, slot_order, block_total)
    slot_len = lookup(hist_len, slot_order, block_total)

    def make_info(offset, count_rows):
        row_ids = offset + jnp.arange(count_rows, dtype=jnp.int32)
        slot_ids = row_ids // row_count
        within = row_ids - slot_ids * row_count
        logical = lookup(slot_order, slot_ids, block_total)
        positions = logical * row_count + within
        hist_ids = lookup(slot_hist, slot_ids, block_total)
        valid_rows = within < lookup(slot_fill, slot_ids, block_total)
        inverse_len = 1.0 / lookup(slot_len, slot_ids, block_total).astype(jnp.float32)
        return (positions, hist_ids, valid_rows, inverse_len)

    own_info = make_info(lax.axis_index("ctx") * row_count, row_count)
    own_query = queries.reshape(row_count, head_count, head_dim)
    own_key = key_rows.reshape(row_count, head_count, head_dim)
    own_value = value_rows.reshape(row_count, head_count, head_dim)
    own_cotan = grad_out.reshape(row_count, head_count, head_dim)

    def query_side(state, piece_key, piece_value, info):
        count_rows = piece_key.shape[0]
        key_part = piece_key.reshape(count_rows, head_count, head_dim)
        value_part = piece_value.reshape(count_rows, head_count, head_dim)
        query_total, rab_total = state
        attn, grad_score, bucket = pair_core(
            own_query, key_part, value_part, own_cotan, own_info, info, rab_table, score_scale
        )
        score_low = grad_score.astype(jnp.bfloat16)
        query_grad = (
            jnp.einsum("hij,jhd->ihd", score_low, key_part, preferred_element_type=jnp.float32)
            * score_scale
        )
        rab_terms = bias_terms(grad_score, bucket, bucket_total)
        return (query_total + query_grad.reshape(row_count, feat_width), rab_total + rab_terms)

    def key_side(state, piece_query, piece_cotan, info):
        count_rows = piece_query.shape[0]
        query_part = piece_query.reshape(count_rows, head_count, head_dim)
        cotan_part = piece_cotan.reshape(count_rows, head_count, head_dim)
        key_total, value_total = state
        attn, grad_score, bucket = pair_core(
            query_part, own_key, own_value, cotan_part, info, own_info, rab_table, score_scale
        )
        key_grad = (
            jnp.einsum(
                "hij,ihd->jhd",
                grad_score.astype(jnp.bfloat16),
                query_part,
                preferred_element_type=jnp.float32,
            )
            * score_scale
        )
        value_grad = jnp.einsum(
            "hij,ihd->jhd",
            attn.astype(jnp.bfloat16),
            cotan_part,
            preferred_element_type=jnp.float32,
        )
        return (
            key_total + key_grad.reshape(row_count, feat_width),
            value_total + value_grad.reshape(row_count, feat_width),
        )

    zero_rows = jnp.zeros((row_count, feat_width), jnp.float32)
    zero_rab = jnp.zeros((head_count, bucket_total), jnp.float32)

    def tile_all(totals, tiles, info):
        tile_query, tile_key, tile_value, tile_cotan = tiles
        query_state = query_side((totals[0], totals[1]), tile_key, tile_value, info)
        key_state = key_side((totals[2], totals[3]), tile_query, tile_cotan, info)
        return (query_state[0], query_state[1], key_state[0], key_state[1])

    pieces = (
        lax.all_gather(queries, "ctx", axis=0, tiled=True),
        lax.all_gather(key_rows, "ctx", axis=0, tiled=True),
        lax.all_gather(value_rows, "ctx", axis=0, tiled=True),
        lax.all_gather(grad_out, "ctx", axis=0, tiled=True),
    )
    tile_count = pieces[0].shape[0] // row_count
    stacked = tuple((piece.reshape(tile_count, row_count, feat_width) for piece in pieces))

    def step(carry, item):
        tile_index = item[0]
        info = make_info(tile_index * row_count, row_count)
        return (tile_all(carry, item[1:], info), None)

    result, unused = lax.scan(
        step,
        (zero_rows, zero_rab, zero_rows, zero_rows),
        (jnp.arange(tile_count, dtype=jnp.int32),) + stacked,
    )
    totals = result
    query_total, rab_total, key_total, value_total = totals
    grad_rab = lax.psum(rab_total, ("dp", "ctx"))
    return (
        query_total.astype(jnp.bfloat16),
        key_total.astype(jnp.bfloat16),
        value_total.astype(jnp.bfloat16),
        grad_rab,
    )


def solution(mesh):
    if mesh.shape["ctx"] == 4:
        body = functools.partial(four_block_device, mesh.shape["dp"])
    else:
        body = scan_device
    return jax.shard_map(
        body,
        mesh=mesh,
        in_specs=(
            P(("dp", "ctx"), None),
            P(("dp", "ctx"), None),
            P(("dp", "ctx"), None),
            P(("dp", "ctx"), None),
            P(),
            P("dp", None),
            P("dp", None),
            P("dp", None),
        ),
        out_specs=(P(("dp", "ctx"), None), P(("dp", "ctx"), None), P(("dp", "ctx"), None), P()),
        check_vma=False,
    )
```
